256 devices in a mesh: context: 64 (over x, z, core), head: 4 (over y).
Axes of the slice: x: 4, y: 4, z: 8, core: 2. Of those that a mesh axis runs over, the one named last changes fastest.
Arguments:
- query_vec: float32 [8192, 4096], P('context', 'head'), may hold values from -6 to 6
- key_vec: float32 [8192, 4096], P('context', 'head'), may hold values from -6 to 6
- value_vec: float32 [8192, 4096], P('context', 'head'), may hold values from -6 to 6
- log_decay: float32 [8192, 4096], P('context', 'head'), may hold values from -0.9 to 0
- beta: float32 [8192, 32], P('context', 'head'), may hold values from 0.5 to 0.95
- latent: bfloat16 [8192, 512], P(('context', 'head')), may hold values from -8 to 8
- latent_query: bfloat16 [8192, 16384], P('context', 'head'), may hold values from -64 to 64
- w_uv: bfloat16 [512, 4096], P(None, 'head'), may hold values from -0.25 to 0.25
- doc_lengths: int32 [128], replicated, may hold values from 1 to 512, 8192 in all
Outputs:
- delta_out: float32 [8192, 4096], P('context', 'head')
- mla_out: bfloat16 [8192, 4096], P('context', 'head')
The draws below stay inside these ranges and needn't reach their ends.
Inputs may be any that keep to these rules, and one draw needn't show every extreme that they name: `doc_lengths`: each document has 1 to 512 tokens, the lengths sum to 8192, and the longest has exactly 512.
All inputs are finite; a program needn't handle non-finite values.
Results may differ from the reference program's by a relative error of at most 0.006.
Values may be sent and summed in bfloat16 or wider, within the bound.
A program may use at most 192 MiB of HBM per device.

```python
import math
import jax
import jax.numpy as jnp
import numpy as np
from jax import lax

HEADS = 32
DK = 128
DV = 128
KV_RANK = 512
TOK_DEV = 128
SPAN = 4
PACKED_TOKENS = 8192
LONGEST_DOCUMENT = 512
NDOCS = 128
N_CONTEXT = 64


def draw_key_vec(key, part):
    key = jax.random.fold_in(key, 11)
    width = HEADS * DK
    groups = PACKED_TOKENS // TOK_DEV
    direction = jax.random.normal(jax.random.fold_in(key, 1), (groups, 1, width), jnp.float32)
    noise = jax.random.normal(jax.random.fold_in(key, 2), (groups, TOK_DEV, width), jnp.float32)
    rows = jnp.clip(direction + 0.5 * noise, -6.0, 6.0)
    return rows.reshape(PACKED_TOKENS, width)


def draw_log_decay(key, part):
    width = HEADS * DK
    fast_share = 0.5
    fast = jax.random.bernoulli(jax.random.fold_in(key, 101), fast_share, (width,))
    slow_rate = jnp.exp(jax.random.uniform(jax.random.fold_in(key, 102), (width,), jnp.float32, jnp.log(0.05 / LONGEST_DOCUMENT), jnp.log(0.5 / LONGEST_DOCUMENT)))
    fast_rate = jax.random.uniform(jax.random.fold_in(key, 103), (width,), jnp.float32, 1.0 / 50.0, 1.0 / 30.0)
    baseline_speed = jnp.where(fast, fast_rate, slow_rate)
    coarse_estimate = jnp.exp(jax.random.uniform(jax.random.fold_in(key, 104), (PACKED_TOKENS, width), jnp.float32, jnp.log(0.5), jnp.log(2.0)))
    current_tier = jnp.exp(jax.random.uniform(jax.random.fold_in(key, 105), (PACKED_TOKENS // TOK_DEV, 1), jnp.float32, jnp.log(0.5), jnp.log(2.0)))
    current_tier = jnp.repeat(current_tier, TOK_DEV, axis=0)
    sudden_spike = jax.random.bernoulli(jax.random.fold_in(key, 106), 3.0 / LONGEST_DOCUMENT, (PACKED_TOKENS, 1))
    training_objective = jax.random.uniform(jax.random.fold_in(key, 107), (PACKED_TOKENS, 1), jnp.float32, 0.2, 0.5)
    return -baseline_speed[None, :] * coarse_estimate * current_tier + jnp.where(sudden_spike, jnp.log(1.0 - training_objective), 0.0)


def latent_pair(key):
    base = jax.random.fold_in(key, 7)
    latent = jnp.clip(jax.random.normal(jax.random.fold_in(base, 1), (PACKED_TOKENS, KV_RANK), jnp.float32), -6.0, 6.0)
    queries = 0.5 * jnp.clip(jax.random.normal(jax.random.fold_in(base, 2), (PACKED_TOKENS, HEADS, KV_RANK), jnp.float32), -6.0, 6.0)
    return (latent, queries.reshape(PACKED_TOKENS, HEADS * KV_RANK))


def draw_latent(key, part):
    return latent_pair(key)[0].astype(jnp.bfloat16)


def draw_latent_query(key, part):
    return latent_pair(key)[1].astype(jnp.bfloat16)


def steps_of(rng, shape, split, smallest, high):
    def one(axis_at, shards_of):
        heights = jax.random.uniform(jax.random.fold_in(jax.random.fold_in(rng, 6), axis_at), (shards_of,), jnp.float32, smallest / len(split), high / len(split))
        return jnp.repeat(jnp.exp(heights), shape[axis_at] // shards_of).reshape((-1,) + (1,) * (len(shape) - axis_at - 1))

    loudness = one(*split[0])
    for cut in split[1:]:
        loudness = loudness * one(*cut)
    return loudness


def profile(amount, total, limit, slope):
    loads = [(1 << 20) // math.isqrt(standing ** slope) + 1 for standing in range(2, amount + 1)]
    surplus, holding = total - limit - (amount - 1), [1] * (amount - 1)
    while surplus > 0:
        movable = [i for i in range(amount - 1) if holding[i] < limit]
        whole, left = sum([loads[i] for i in movable]), surplus
        for i in movable:
            extra = min(limit - holding[i], max(1, left * loads[i] // whole), surplus)
            holding[i] = holding[i] + extra
            surplus = surplus - extra
    return np.array([limit] + holding)


def ragged(key, count, total, limit, skew):
    if count == 2:
        one = jax.random.randint(key, (), max(1, total - limit), min(limit, total - 1) + 1)
        return jnp.stack([one, total - one])
    lengths = jnp.asarray(profile(count, total, limit, skew), jnp.int32)
    pairs = (count - 1) // 2
    giver, taker = lengths[1:1 + 2 * pairs:2], lengths[2:2 + 2 * pairs:2]
    margin = jnp.minimum(giver - 1, limit - taker)
    passed = jax.random.randint(jax.random.fold_in(key, 1), (pairs,), 0, 1 << 20) % (margin + 1)
    lengths = lengths.at[1:1 + 2 * pairs:2].set(giver - passed).at[2:2 + 2 * pairs:2].set(taker + passed)
    return lengths[jax.random.permutation(jax.random.fold_in(key, 2), count)]


def centred(key, shape, scale, bound, pieces=(), kind=jnp.bfloat16):
    entries = scale * jax.random.normal(key, shape, jnp.float32)
    if pieces:
        entries = entries * steps_of(key, shape, pieces, -0.22, 0.18)
    return jnp.clip(entries, -bound, bound).astype(kind)


def setup_inputs(seed: int = 0) -> dict:
    seeds = jax.random.split(jax.random.key(seed), 10)
    query_vec = centred(seeds[0], (PACKED_TOKENS, HEADS * DK), 1.0, 6.0, ((0, 64), (1, 4)), jnp.float32)
    key_vec = draw_key_vec(jax.random.fold_in(seeds[9], 71), 0)
    value_vec = centred(seeds[2], (PACKED_TOKENS, HEADS * DV), 1.0, 6.0, ((0, 64), (1, 4)), jnp.float32)
    log_decay = draw_log_decay(jax.random.fold_in(seeds[9], 71), 0)
    beta = jnp.clip(0.5 + 0.45 * jax.random.uniform(seeds[4], (PACKED_TOKENS, HEADS), jnp.float32) ** steps_of(seeds[4], (PACKED_TOKENS, HEADS), ((0, 64), (1, 4)), -0.2, 0.2), 0.5, 0.95)
    latent = draw_latent(jax.random.fold_in(seeds[9], 71), 0)
    latent_query = draw_latent_query(jax.random.fold_in(seeds[9], 71), 0)
    w_uv = centred(seeds[7], (KV_RANK, HEADS * DV), KV_RANK ** -0.5, 0.25, ((1, 4),))
    doc_lengths = ragged(seeds[8], NDOCS, PACKED_TOKENS, LONGEST_DOCUMENT, 2).astype(jnp.int32)
    return {"query_vec": query_vec, "key_vec": key_vec, "value_vec": value_vec, "log_decay": log_decay, "beta": beta, "latent": latent, "latent_query": latent_query, "w_uv": w_uv, "doc_lengths": doc_lengths}


UPPER_LIMIT = lax.Precision.HIGHEST
FAR = -1e+30

def doc_starts(doc_lengths, positions):
    endings = jnp.cumsum(doc_lengths).astype(jnp.int32)
    beginnings = (endings - doc_lengths).astype(jnp.int32)
    covered = beginnings[None, :] <= positions[:, None]
    return lax.optimization_barrier(jnp.max(jnp.where(covered, beginnings[None, :], -1), axis=1)).astype(jnp.int32)

def unit_rows(matrix):
    return matrix * lax.rsqrt(lax.optimization_barrier(jnp.sum(matrix * matrix, axis=-1, keepdims=True)) + 1e-06)

def reference(query_vec, key_vec, value_vec, log_decay, beta, latent, latent_query, w_uv, doc_lengths):
    positions = jnp.arange(PACKED_TOKENS, dtype=jnp.int32)
    token_start = doc_starts(doc_lengths, positions)
    restart = token_start == positions
    unit_query = unit_rows(query_vec.reshape(PACKED_TOKENS, HEADS, DK))
    unit_key = unit_rows(key_vec.reshape(PACKED_TOKENS, HEADS, DK))
    values_in = value_vec.reshape(PACKED_TOKENS, HEADS, DV)
    decay = jnp.exp(log_decay.reshape(PACKED_TOKENS, HEADS, DK))

    def advance(present_state, inputs):
        query_current, key_current, value_t, decay_t, beta_t, restart_t = inputs
        present_state = jnp.where(restart_t, 0.0, present_state) * decay_t[:, :, None]
        retrieved_memory = jnp.einsum('qoa,qo->qa', present_state, key_current, precision=UPPER_LIMIT)
        update = beta_t[:, None] * (value_t - retrieved_memory)
        present_state = present_state + key_current[:, :, None] * update[:, None, :]
        return (present_state, jnp.einsum('qoa,qo->qa', present_state, query_current, precision=UPPER_LIMIT))
    initial = jnp.zeros((HEADS, DK, DV), jnp.float32)
    _, delta_rows = lax.scan(advance, initial, (unit_query, unit_key, values_in, decay, beta, restart))
    delta_out = delta_rows.reshape(PACKED_TOKENS, HEADS * DV)
    queries = latent_query.reshape(PACKED_TOKENS, HEADS, KV_RANK)
    up_proj = w_uv.reshape(KV_RANK, HEADS, DV).astype(jnp.float32)
    span_len = (SPAN + 1) * TOK_DEV
    scale = DK ** (-0.5)

    def attend(block_idx):
        query_lo = (block_idx * TOK_DEV).astype(jnp.int32)
        key_lo = jnp.clip(query_lo - SPAN * TOK_DEV, 0, PACKED_TOKENS - span_len).astype(jnp.int32)
        query_blk = lax.dynamic_slice_in_dim(queries, query_lo, TOK_DEV, 0).astype(jnp.float32)
        key_blk = lax.dynamic_slice_in_dim(latent, key_lo, span_len, 0).astype(jnp.float32)
        query_pos = query_lo + jnp.arange(TOK_DEV, dtype=jnp.int32)
        key_pos = key_lo + jnp.arange(span_len, dtype=jnp.int32)
        query_doc = lax.dynamic_slice_in_dim(token_start, query_lo, TOK_DEV, 0)
        key_doc = lax.dynamic_slice_in_dim(token_start, key_lo, span_len, 0)
        visible = (query_doc[:, None] == key_doc[None, :]) & (key_pos[None, :] <= query_pos[:, None])
        scores = jnp.einsum('thr,kr->thk', query_blk, key_blk, precision=UPPER_LIMIT) * scale
        scores = jnp.where(visible[:, None, :], scores, FAR)
        row_top = lax.optimization_barrier(jnp.max(scores, axis=-1, keepdims=True))
        exponent = jnp.where(visible[:, None, :], jnp.exp(scores - row_top), 0.0)
        totals = lax.optimization_barrier(jnp.sum(exponent, axis=-1, keepdims=True))
        weights = lax.optimization_barrier(exponent.astype(jnp.bfloat16)).astype(jnp.float32)
        context_vec = jnp.einsum('thk,kr->thr', weights, key_blk, precision=UPPER_LIMIT) / totals
        context_vec = lax.optimization_barrier(context_vec.astype(jnp.bfloat16)).astype(jnp.float32)
        mixed = jnp.einsum('thr,rhd->thd', context_vec, up_proj, precision=UPPER_LIMIT)
        return mixed.astype(jnp.bfloat16).reshape(TOK_DEV, HEADS * DV)
    mla_out = lax.map(attend, jnp.arange(N_CONTEXT, dtype=jnp.int32)).reshape(PACKED_TOKENS, HEADS * DV)
    return (delta_out, mla_out)
```

```python
import functools

import jax
import jax.numpy as jnp
from jax import lax
from jax.experimental import pallas as pl
from jax.experimental.pallas import tpu as pltpu
from jax.sharding import PartitionSpec as P

MESH = pl.DeviceIdType.MESH
F32 = jnp.float32
BF16 = jnp.bfloat16
FAR = -1e30
EPS = 1e-6
SPAN = 4
TOK = 128
WIDTH = 128
GROUP = 4
LEVELS = 7


def mul(left, right):
    return lax.dot_general(left, right, (((1,), (0,)), ((), ())), preferred_element_type=F32)


def mul_nt(left, right):
    return lax.dot_general(left, right, (((1,), (1,)), ((), ())), preferred_element_type=F32)


def mul_tn(left, right):
    return lax.dot_general(left, right, (((0,), (0,)), ((), ())), preferred_element_type=F32)


def halves(matrix):
    high = matrix.astype(BF16)
    return high, (matrix - high.astype(F32)).astype(BF16)


def three(product, left, right):
    return product(left[0], right[0]) + product(left[1], right[0]) + product(left[0], right[1])


def iota2(shape, axis):
    return lax.broadcasted_iota(jnp.int32, shape, axis)


def prepare_masks(lens, shard, pair_mask, link_mask, level_mask, bias):
    square = (TOK, TOK)
    row, col = iota2(square, 0), iota2(square, 1)
    lens_f = lens.astype(F32)
    lens_row = jnp.broadcast_to(lens_f, square)
    begin_col = jnp.sum(jnp.where(col < row, lens_row, 0.0), axis=1, keepdims=True)
    lens_col = jnp.sum(jnp.where(col == row, lens_row, 0.0), axis=1, keepdims=True)
    begin_row = jnp.sum(jnp.where(row < col, lens_col, 0.0), axis=0, keepdims=True)
    low = shard * TOK
    pos_col = (low + iota2((TOK, 1), 0)).astype(F32)
    start_col = jnp.max(jnp.where(begin_row <= pos_col, begin_row, -1.0), axis=1, keepdims=True)
    keys = (SPAN + 1) * TOK
    pos_row = (low - SPAN * TOK + iota2((1, keys), 1)).astype(F32)
    start_row = jnp.max(jnp.where(begin_col <= pos_row, begin_col, -1.0), axis=0, keepdims=True)
    visible = (start_col == start_row) & (pos_row <= pos_col)
    bias[...] = jnp.where(visible, 0.0, FAR)
    same = start_col == start_row[:, SPAN * TOK :]
    pair_mask[0] = jnp.where(same & (row >= col), 1.0, 0.0)
    pair_mask[1] = jnp.where(same & (row > col), 1.0, 0.0)
    link_mask[0] = jnp.broadcast_to(jnp.where(start_col < low.astype(F32), 1.0, 0.0), square)
    link_mask[1] = jnp.broadcast_to(jnp.where(start_col == start_col[TOK - 1 :, :], 1.0, 0.0), square)
    for level in range(LEVELS):
        below = ((row >> (level + 1)) == (col >> (level + 1))) & ((row >> level) > (col >> level))
        level_mask[level] = jnp.where(below, 1.0, 0.0).astype(BF16)
    level_mask[LEVELS] = jnp.where(row == col, 1.0, 0.0).astype(BF16)


def delta_local(first, heads, refs, pair_mask, link_mask, level_mask, a_ref, c_ref, left_ref, base_ref):
    query_ref, key_ref, value_ref, decay_ref, beta_ref = refs
    square = (TOK, TOK)
    row, col = iota2(square, 0), iota2(square, 1)
    lower = jnp.where(row >= col, 1.0, 0.0).astype(BF16)
    incl, strict = pair_mask[0] > 0.5, pair_mask[1] > 0.5
    link, tail = link_mask[0], link_mask[1]
    link_last = link[TOK - 1 :, :]
    beta_all = beta_ref[...]
    beta_col = iota2(beta_all.shape, 1)
    span = range(heads)
    lanes = [pl.ds(pl.multiple_of((first + h) * WIDTH, WIDTH), WIDTH) for h in span]
    solve, weight, q_in, tail_t, right, end_row = [], [], [], [], [], []
    for h in span:
        decay = decay_ref[:, lanes[h]]
        high, rest = decay.astype(BF16), None
        rest = decay - high.astype(F32)
        mid = rest.astype(BF16)
        low = (rest - mid.astype(F32)).astype(BF16)
        cum = mul(lower, high) + mul(lower, mid) + mul(lower, low)
        centre, end = cum[TOK // 2 - 1 : TOK // 2, :], cum[TOK - 1 :, :]
        grow, shrink = jnp.exp(cum - centre), jnp.exp(centre - cum)
        from_start, to_end = jnp.exp(centre), jnp.exp(end - centre)
        query, key = query_ref[:, lanes[h]], key_ref[:, lanes[h]]
        query = query * lax.rsqrt(jnp.sum(query * query, axis=1, keepdims=True) + EPS)
        key = key * lax.rsqrt(jnp.sum(key * key, axis=1, keepdims=True) + EPS)
        query_grow, key_grow, key_shrink = query * grow, key * grow, key * shrink
        pairs = three(
            mul_nt, halves(jnp.concatenate([query_grow, key_grow], axis=0)), halves(key_shrink)
        )
        beta = jnp.sum(jnp.where(beta_col == first + h, beta_all, 0.0), axis=1, keepdims=True)
        weight.append(halves(jnp.where(incl, pairs[:TOK], 0.0)))
        solve.append(halves(jnp.where(strict, pairs[TOK:], 0.0) * beta))
        in_scale = link * from_start
        q_in.append(query_grow * in_scale)
        right.append(
            jnp.concatenate([value_ref[:, lanes[h]] * beta, key_grow * in_scale * beta], axis=1)
        )
        tail_t.append(halves(key_shrink * (tail * to_end)))
        end_row.append(jnp.exp(end) * link_last)
    inverse = [level_mask[LEVELS] - solve[h][0] * level_mask[0] for h in span]
    for level in range(1, LEVELS):
        part = [mul(solve[h][0] * level_mask[level], inverse[h]).astype(BF16) for h in span]
        inverse = [inverse[h] - mul(inverse[h], part[h]).astype(BF16) for h in span]
    solved = [mul(inverse[h], right[h].astype(BF16)) for h in span]
    rest = [right[h] - solved[h] - three(mul, solve[h], halves(solved[h])) for h in span]
    solved = [halves(solved[h] + mul(inverse[h], rest[h].astype(BF16))) for h in span]
    for h in span:
        change = three(mul_tn, tail_t[h], solved[h])
        output = three(mul, weight[h], solved[h])
        c_ref[first + h] = change[:, :WIDTH]
        a_ref[first + h] = (jnp.where(row == col, end_row[h], 0.0) - change[:, WIDTH:]).astype(BF16)
        base_ref[:, lanes[h]] = output[:, :WIDTH]
        left_ref[first + h] = (q_in[h] - output[:, WIDTH:]).astype(BF16)


def latent_part(first, heads, scale, query_rows, keys, bias, up_ref, out_ref):
    rows = heads * TOK
    scores = mul_nt(query_rows[first * TOK : first * TOK + rows, :], keys[...])
    mask = jnp.concatenate([bias[...]] * heads, axis=0)
    scores = scores * scale + mask
    top = jnp.max(scores, axis=1, keepdims=True)
    weights = jnp.exp(scores - top)
    totals = jnp.sum(weights, axis=1, keepdims=True)
    context = mul(weights.astype(BF16), keys[...]) * (1.0 / totals)
    context = context.astype(BF16)
    for h in range(heads):
        at = (first + h) * WIDTH
        out_ref[:, at : at + WIDTH] = mul(
            context[h * TOK : (h + 1) * TOK], up_ref[:, at : at + WIDTH]
        ).astype(BF16)


def body(
    shards, head_devices, heads, scale,
    query_hbm, key_hbm, value_hbm, decay_hbm, beta_ref, latent_hbm, latq_hbm, up_hbm, lens_ref,
    delta_hbm, mla_hbm,
    query_v, key_v, value_v, decay_v, latq_v, up_v, keys, base, mla_v,
    pair_mask, link_mask, level_mask, bias,
    a_ref, c_ref, left_ref, send_buf, recv_buf,
    load_sem, store_sem, chain_send, chain_recv, near_send, near_recv, side_send, side_recv, twin_send, twin_recv,
):
    shard = lax.axis_index("context")
    side = lax.axis_index("head")
    core = lax.rem(shard, 2)
    rank = latq_v.shape[1]
    quarter = TOK // head_devices

    def behind(steps):
        return lax.rem(shard + shards + steps, shards)

    def block_rows(block, place):
        return pl.ds(pl.multiple_of(block * TOK + place * quarter, quarter), quarter)

    loads = [
        pltpu.make_async_copy(source, target, load_sem.at[i])
        for i, (source, target) in enumerate(
            [(decay_hbm, decay_v), (key_hbm, key_v), (query_hbm, query_v), (value_hbm, value_v), (up_hbm, up_v)]
        )
    ]
    for h in range(heads):
        loads.append(
            pltpu.make_async_copy(
                latq_hbm.at[:, pl.ds(h * rank, rank)], latq_v.at[pl.ds(h * TOK, TOK), :], load_sem.at[5 + h]
            )
        )
    own = pltpu.make_async_copy(latent_hbm, keys.at[block_rows(SPAN, side)], load_sem.at[5 + heads])
    own.start()
    for load in loads:
        load.start()

    barrier = pltpu.get_barrier_semaphore()
    peers = [(behind(steps), side) for steps in (1, -1, 2, -2, 4, -4)]
    peers += [(shard, lax.rem(side + step, head_devices)) for step in range(1, head_devices)]
    for peer in peers:
        pl.semaphore_signal(barrier, inc=1, device_id=peer, device_id_type=MESH)
    pl.semaphore_wait(barrier, len(peers))

    def near_copy(i):
        steps = (2, 4)[i]
        return pltpu.make_async_remote_copy(
            src_ref=latent_hbm, dst_ref=keys.at[block_rows(SPAN - steps, side)],
            send_sem=near_send.at[i], recv_sem=near_recv.at[i],
            device_id=(behind(steps), side), device_id_type=MESH,
        )

    def side_copy(i, step):
        place = block_rows(SPAN - 2 * i, side)
        at = i * (head_devices - 1) + step - 1
        return pltpu.make_async_remote_copy(
            src_ref=keys.at[place], dst_ref=keys.at[place],
            send_sem=side_send.at[at], recv_sem=side_recv.at[at],
            device_id=(shard, lax.rem(side + step, head_devices)), device_id_type=MESH,
        )

    def side_arrival(i, step):
        place = block_rows(SPAN - 2 * i, lax.rem(side + head_devices - step, head_devices))
        at = i * (head_devices - 1) + step - 1
        return pltpu.make_async_remote_copy(
            src_ref=keys.at[place], dst_ref=keys.at[place],
            send_sem=side_send.at[at], recv_sem=side_recv.at[at],
            device_id=(shard, lax.rem(side + step, head_devices)), device_id_type=MESH,
        )

    def twin_copy(i):
        source = pl.ds(pl.multiple_of((2 * i + 2 * (1 - core)) * TOK, TOK), TOK)
        return pltpu.make_async_remote_copy(
            src_ref=keys.at[source], dst_ref=keys.at[pl.ds((2 * i + 1) * TOK, TOK)],
            send_sem=twin_send.at[i], recv_sem=twin_recv.at[i],
            device_id=(shard + 1 - 2 * core, side), device_id_type=MESH,
        )

    def chain_copy(step, h):
        return pltpu.make_async_remote_copy(
            src_ref=send_buf.at[step, h], dst_ref=recv_buf.at[step, h],
            send_sem=chain_send.at[step, h], recv_sem=chain_recv.at[step, h],
            device_id=(behind(1), side), device_id_type=MESH,
        )

    def chain_first(first, count):
        @pl.when(core == 0)
        def _():
            for h in range(first, first + count):
                send_buf[0, h] = c_ref[h].astype(BF16)
                chain_copy(0, h).start()

    def chain_second(first, count):
        @pl.when(core == 1)
        def _():
            for h in range(first, first + count):
                chain_copy(0, h).wait_recv()
                joined = c_ref[h] + mul(a_ref[h], recv_buf[0, h])
                c_ref[h] = joined
                send_buf[0, h] = joined.astype(BF16)
                chain_copy(0, h).start()

    def chain_third(first, count):
        @pl.when(core == 0)
        def _():
            for h in range(first, first + count):
                chain_copy(0, h).wait_recv()
                send_buf[1, h] = mul(a_ref[h], recv_buf[0, h]).astype(BF16)
                chain_copy(1, h).start()

    def chain_fourth(first, count):
        @pl.when(core == 1)
        def _():
            for h in range(first, first + count):
                chain_copy(1, h).wait_recv()
                send_buf[1, h] = (c_ref[h] + mul(a_ref[h], recv_buf[1, h])).astype(BF16)
                chain_copy(1, h).start()

    def emit(h, incoming):
        at = h * WIDTH
        base[:, at : at + WIDTH] += mul(left_ref[h], incoming)

    def chain_fifth(first, count):
        @pl.when(core == 0)
        def _():
            for h in range(first, first + count):
                chain_copy(1, h).wait_recv()
                send_buf[2, h] = (c_ref[h] + mul(a_ref[h], recv_buf[1, h])).astype(BF16)
                chain_copy(2, h).start()
                emit(h, recv_buf[1, h])

    def chain_sixth(first, count):
        @pl.when(core == 1)
        def _():
            for h in range(first, first + count):
                chain_copy(2, h).wait_recv()
                emit(h, recv_buf[2, h])

    for i in range(2):
        near_copy(i).start()
    own.wait()
    for step in range(1, head_devices):
        side_copy(0, step).start()

    prepare_masks(lens_ref[...], shard, pair_mask, link_mask, level_mask, bias)
    for load in loads[:4]:
        load.wait()
    refs = (query_v, key_v, value_v, decay_v, beta_ref)
    delta_local(0, GROUP, refs, pair_mask, link_mask, level_mask, a_ref, c_ref, left_ref, base)
    chain_first(0, GROUP)
    for i in range(2):
        near_copy(i).wait_recv()
        for step in range(1, head_devices):
            side_copy(i + 1, step).start()
    delta_local(GROUP, GROUP, refs, pair_mask, link_mask, level_mask, a_ref, c_ref, left_ref, base)
    chain_first(GROUP, GROUP)
    chain_second(0, heads)
    for i in range(SPAN // 2 + 1):
        for step in range(1, head_devices):
            side_arrival(i, step).wait_recv()
    for i in range(2):
        twin_copy(i).start()
    for load in loads[4:]:
        load.wait()
    for i in range(2):
        twin_copy(i).wait_recv()

    def latent_at(part):
        latent_part(part * 2, 2, scale, latq_v, keys, bias, up_v, mla_v)

    latent_at(0)
    chain_third(0, heads)
    latent_at(1)
    chain_fourth(0, heads)
    latent_at(2)
    chain_fifth(0, heads)
    latent_at(3)
    mla_out = pltpu.make_async_copy(mla_v, mla_hbm, store_sem.at[0])
    mla_out.start()
    chain_sixth(0, heads)
    delta_out = pltpu.make_async_copy(base, delta_hbm, store_sem.at[1])
    delta_out.start()
    for i in range(2):
        near_copy(i).wait_send()
        twin_copy(i).wait_send()
    for i in range(SPAN // 2 + 1):
        for step in range(1, head_devices):
            side_copy(i, step).wait_send()
    for h in range(heads):
        for step in range(2):
            chain_copy(step, h).wait_send()

    @pl.when(core == 0)
    def _():
        for h in range(heads):
            chain_copy(2, h).wait_send()

    mla_out.wait()
    delta_out.wait()


def solution(mesh):
    shards = mesh.shape["context"]
    head_devices = mesh.shape["head"]

    def step(query_vec, key_vec, value_vec, log_decay, beta, latent, latent_query, w_uv, doc_lengths):
        rows = query_vec.shape[0]
        heads = beta.shape[1]
        rank = w_uv.shape[0]
        width = query_vec.shape[1]
        keys = (SPAN + 1) * rows
        square = (rows, rows)
        anywhere = pl.BlockSpec(memory_space=pl.ANY)
        inside = pl.BlockSpec(memory_space=pltpu.VMEM)
        dma = pltpu.SemaphoreType.DMA
        side_copies = (SPAN // 2 + 1) * (head_devices - 1)
        return pl.pallas_call(
            functools.partial(body, shards, head_devices, heads, WIDTH**-0.5),
            out_shape=(
                jax.ShapeDtypeStruct((rows, width), F32),
                jax.ShapeDtypeStruct((rows, width), BF16),
            ),
            in_specs=[anywhere] * 4 + [inside] + [anywhere] * 3 + [inside],
            out_specs=(anywhere, anywhere),
            scratch_shapes=[
                pltpu.VMEM((rows, width), F32),
                pltpu.VMEM((rows, width), F32),
                pltpu.VMEM((rows, width), F32),
                pltpu.VMEM((rows, width), F32),
                pltpu.VMEM((rows * heads, rank), BF16),
                pltpu.VMEM((rank, width), BF16),
                pltpu.VMEM((keys, rank), BF16),
                pltpu.VMEM((rows, width), F32),
                pltpu.VMEM((rows, width), BF16),
                pltpu.VMEM((2,) + square, F32),
                pltpu.VMEM((2,) + square, F32),
                pltpu.VMEM((LEVELS + 1,) + square, BF16),
                pltpu.VMEM((rows, keys), F32),
                pltpu.VMEM((heads,) + square, BF16),
                pltpu.VMEM((heads,) + square, F32),
                pltpu.VMEM((heads,) + square, BF16),
                pltpu.VMEM((3, heads) + square, BF16),
                pltpu.VMEM((3, heads) + square, BF16),
                dma((6 + heads,)),
                dma((2,)),
                dma((3, heads)),
                dma((3, heads)),
                dma((2,)),
                dma((2,)),
                dma((side_copies,)),
                dma((side_copies,)),
                dma((2,)),
                dma((2,)),
            ],
            compiler_params=pltpu.CompilerParams(
                collective_id=0, has_side_effects=True, vmem_limit_bytes=48 * 1024 * 1024
            ),
            cost_estimate=pl.CostEstimate(flops=3_000_000_000, bytes_accessed=6_000_000, transcendentals=1_000_000),
            name="packed_attention",
        )(
            query_vec, key_vec, value_vec, log_decay, beta, latent, latent_query, w_uv,
            doc_lengths.reshape(1, -1),
        )

    return jax.shard_map(
        step,
        mesh=mesh,
        in_specs=(
            P("context", "head"),
            P("context", "head"),
            P("context", "head"),
            P("context", "head"),
            P("context", "head"),
            P(("context", "head"), None),
            P("context", "head"),
            P(None, "head"),
            P(),
        ),
        out_specs=(P("context", "head"), P("context", "head")),
        check_vma=False,
    )
```

```python
import functools

import jax
import jax.numpy as jnp
from jax import lax
from jax.experimental import pallas as pl
from jax.experimental.pallas import tpu as pltpu
from jax.sharding import PartitionSpec as P

MESH = pl.DeviceIdType.MESH
F32 = jnp.float32
BF16 = jnp.bfloat16
FAR = -1e30
EPS = 1e-6
SPAN = 4
TOK = 128
WIDTH = 128
LEVELS = 7


def mul(left, right):
    return lax.dot_general(left, right, (((1,), (0,)), ((), ())), preferred_element_type=F32)


def mul_nt(left, right):
    return lax.dot_general(left, right, (((1,), (1,)), ((), ())), preferred_element_type=F32)


def mul_tn(left, right):
    return lax.dot_general(left, right, (((0,), (0,)), ((), ())), preferred_element_type=F32)


def halves(matrix):
    high = matrix.astype(BF16)
    return high, (matrix - high.astype(F32)).astype(BF16)


def three(product, left, right):
    return product(left[0], right[0]) + product(left[1], right[0]) + product(left[0], right[1])


def iota2(shape, axis):
    return lax.broadcasted_iota(jnp.int32, shape, axis)


def prepare_masks(lens, shard, pair_mask, link_mask, level_mask, bias):
    square = (TOK, TOK)
    row, col = iota2(square, 0), iota2(square, 1)
    lens_f = lens.astype(F32)
    lens_row = jnp.broadcast_to(lens_f, square)
    begin_col = jnp.sum(jnp.where(col < row, lens_row, 0.0), axis=1, keepdims=True)
    lens_col = jnp.sum(jnp.where(col == row, lens_row, 0.0), axis=1, keepdims=True)
    begin_row = jnp.sum(jnp.where(row < col, lens_col, 0.0), axis=0, keepdims=True)
    low = shard * TOK
    pos_col = (low + iota2((TOK, 1), 0)).astype(F32)
    start_col = jnp.max(jnp.where(begin_row <= pos_col, begin_row, -1.0), axis=1, keepdims=True)
    keys = (SPAN + 1) * TOK
    pos_row = (low - SPAN * TOK + iota2((1, keys), 1)).astype(F32)
    start_row = jnp.max(jnp.where(begin_col <= pos_row, begin_col, -1.0), axis=0, keepdims=True)
    visible = (start_col == start_row) & (pos_row <= pos_col)
    bias[...] = jnp.where(visible, 0.0, FAR)
    same = start_col == start_row[:, SPAN * TOK :]
    pair_mask[0] = jnp.where(same & (row >= col), 1.0, 0.0)
    pair_mask[1] = jnp.where(same & (row > col), 1.0, 0.0)
    link_mask[0] = jnp.broadcast_to(jnp.where(start_col < low.astype(F32), 1.0, 0.0), square)
    link_mask[1] = jnp.broadcast_to(jnp.where(start_col == start_col[TOK - 1 :, :], 1.0, 0.0), square)
    for level in range(LEVELS):
        below = ((row >> (level + 1)) == (col >> (level + 1))) & ((row >> level) > (col >> level))
        level_mask[level] = jnp.where(below, 1.0, 0.0).astype(BF16)
    level_mask[LEVELS] = jnp.where(row == col, 1.0, 0.0).astype(BF16)


def delta_pairs(heads, refs, pair_mask, link_mask):
    query_ref, key_ref, value_ref, decay_ref, beta_ref = refs
    square = (TOK, TOK)
    row, col = iota2(square, 0), iota2(square, 1)
    lower = jnp.where(row >= col, 1.0, 0.0).astype(BF16)
    incl, strict = pair_mask[0] > 0.5, pair_mask[1] > 0.5
    link, tail = link_mask[0], link_mask[1]
    link_last = link[TOK - 1 :, :]
    beta_cols = beta_ref[...].T
    parts = []
    for h in range(heads):
        lanes = slice(h * WIDTH, (h + 1) * WIDTH)
        decay = decay_ref[:, lanes]
        high = decay.astype(BF16)
        rest = decay - high.astype(F32)
        mid = rest.astype(BF16)
        low = (rest - mid.astype(F32)).astype(BF16)
        cum = mul(lower, high) + mul(lower, mid) + mul(lower, low)
        centre, end = cum[TOK // 2 - 1 : TOK // 2, :], cum[TOK - 1 :, :]
        grow, shrink = jnp.exp(cum - centre), jnp.exp(centre - cum)
        from_start, to_end = jnp.exp(centre), jnp.exp(end - centre)
        query, key = query_ref[:, lanes], key_ref[:, lanes]
        query = query * lax.rsqrt(jnp.sum(query * query, axis=1, keepdims=True) + EPS)
        key = key * lax.rsqrt(jnp.sum(key * key, axis=1, keepdims=True) + EPS)
        query_grow, key_grow, key_shrink = query * grow, key * grow, key * shrink
        pairs = three(
            mul_nt, halves(jnp.concatenate([query_grow, key_grow], axis=0)), halves(key_shrink)
        )
        beta = beta_cols[:, h : h + 1]
        in_scale = link * from_start
        parts.append(
            dict(
                weight=halves(jnp.where(incl, pairs[:TOK], 0.0)),
                system=halves(jnp.where(strict, pairs[TOK:], 0.0) * beta),
                query_in=query_grow * in_scale,
                right=jnp.concatenate(
                    [value_ref[:, lanes] * beta, key_grow * in_scale * beta], axis=1
                ),
                tail=halves(key_shrink * (tail * to_end)),
                end=jnp.exp(end) * link_last,
            )
        )
    return parts


def delta_solve(parts, level_mask, a_ref, c_ref):
    square = (TOK, TOK)
    row, col = iota2(square, 0), iota2(square, 1)
    system = [part["system"] for part in parts]
    right = [part["right"] for part in parts]
    span = range(len(parts))
    inverse = [level_mask[LEVELS] - system[h][0] * level_mask[0] for h in span]
    for level in range(1, LEVELS):
        inner = [mul(system[h][0] * level_mask[level], inverse[h]).astype(BF16) for h in span]
        inverse = [inverse[h] - mul(inverse[h], inner[h]).astype(BF16) for h in span]
    solved = [mul(inverse[h], right[h].astype(BF16)) for h in span]
    rest = [right[h] - solved[h] - three(mul, system[h], halves(solved[h])) for h in span]
    solved = [halves(solved[h] + mul(inverse[h], rest[h].astype(BF16))) for h in span]
    for h in span:
        change = three(mul_tn, parts[h]["tail"], solved[h])
        c_ref[h] = change[:, :WIDTH]
        a_ref[h] = (jnp.where(row == col, parts[h]["end"], 0.0) - change[:, WIDTH:]).astype(BF16)
    return solved


def delta_outputs(parts, solved, left_ref, base_ref):
    for h in range(len(parts)):
        output = three(mul, parts[h]["weight"], solved[h])
        base_ref[:, h * WIDTH : (h + 1) * WIDTH] = output[:, :WIDTH]
        left_ref[h] = (parts[h]["query_in"] - output[:, WIDTH:]).astype(BF16)


def latent_part(first, heads, scale, query_rows, keys, bias, up_ref, out_ref):
    rows = heads * TOK
    scores = mul_nt(query_rows[first * TOK : first * TOK + rows, :], keys[...])
    mask = jnp.concatenate([bias[...]] * heads, axis=0)
    scores = scores * scale + mask
    top = jnp.max(scores, axis=1, keepdims=True)
    weights = jnp.exp(scores - top)
    totals = jnp.sum(weights, axis=1, keepdims=True)
    context = mul(weights.astype(BF16), keys[...]) * (1.0 / totals)
    context = context.astype(BF16)
    for h in range(heads):
        at = (first + h) * WIDTH
        out_ref[:, at : at + WIDTH] = mul(
            context[h * TOK : (h + 1) * TOK], up_ref[:, at : at + WIDTH]
        ).astype(BF16)


def body(
    shards, head_devices, heads, scale,
    query_hbm, key_hbm, value_hbm, decay_hbm, beta_hbm, latent_hbm, latq_hbm, up_hbm, lens_hbm,
    base, mla_v,
    query_v, key_v, value_v, decay_v, beta_v, latq_v, up_v, keys, lens_v,
    pair_mask, link_mask, level_mask, bias,
    a_ref, c_ref, left_ref, step_ref, send_buf, recv_buf,
    load_sem, chain_send, chain_recv, near_send, near_recv, side_send, side_recv, twin_send, twin_recv,
):
    shard = lax.axis_index("context")
    side = lax.axis_index("head")
    core = lax.rem(shard, 2)
    chip = shard // 2
    last = shards // 2 - 1
    is_a, is_b = core == 0, core == 1
    rank = latq_v.shape[1]
    quarter = TOK // head_devices
    near = (2, 4)

    def ahead(steps):
        return lax.rem(shard + shards + steps, shards)

    def block_rows(block, place):
        return pl.ds(pl.multiple_of(block * TOK + place * quarter, quarter), quarter)

    pairs = [(lens_hbm, lens_v), (decay_hbm, decay_v), (key_hbm, key_v), (query_hbm, query_v)]
    pairs += [(value_hbm, value_v), (beta_hbm, beta_v), (up_hbm, up_v)]
    pairs += [
        (latq_hbm.at[:, pl.ds(h * rank, rank)], latq_v.at[pl.ds(h * TOK, TOK), :]) for h in range(heads)
    ]
    pairs += [(latent_hbm, keys.at[block_rows(SPAN, side)])]
    loads = [pltpu.make_async_copy(pairs[i][0], pairs[i][1], load_sem.at[i]) for i in range(len(pairs))]
    loads[0].start()
    loads[-1].start()
    for load in loads[1:-1]:
        load.start()

    barrier = pltpu.get_barrier_semaphore()

    def greet(peer):
        pl.semaphore_signal(barrier, inc=1, device_id=peer, device_id_type=MESH)

    for step in range(1, head_devices):
        greet((shard, lax.rem(side + step, head_devices)))
    for steps in (1,) + near:
        @pl.when(shard >= steps)
        def _(steps=steps):
            greet((ahead(-steps), side))

    @pl.when(is_a)
    def _():
        greet((ahead(1), side))

    def one_if(condition):
        return jnp.where(condition, 1, 0).astype(jnp.int32)

    expected = head_devices - 1 + core
    for steps in (1,) + near:
        expected = expected + one_if(shard + steps < shards)

    def near_copy(i):
        return pltpu.make_async_remote_copy(
            src_ref=latent_hbm, dst_ref=keys.at[block_rows(SPAN - near[i], side)],
            send_sem=near_send.at[i], recv_sem=near_recv.at[i],
            device_id=(ahead(near[i]), side), device_id_type=MESH,
        )

    def side_copy(i, step, place):
        rows = block_rows(SPAN - 2 * i, place)
        at = i * (head_devices - 1) + step - 1
        return pltpu.make_async_remote_copy(
            src_ref=keys.at[rows], dst_ref=keys.at[rows],
            send_sem=side_send.at[at], recv_sem=side_recv.at[at],
            device_id=(shard, lax.rem(side + step, head_devices)), device_id_type=MESH,
        )

    def side_start(i):
        for step in range(1, head_devices):
            side_copy(i, step, side).start()

    def side_arrived(i):
        for step in range(1, head_devices):
            side_copy(i, step, lax.rem(side + head_devices - step, head_devices)).wait_recv()

    def twin_copy(i):
        source = pl.ds(pl.multiple_of((2 * i + 2 * (1 - core)) * TOK, TOK), TOK)
        return pltpu.make_async_remote_copy(
            src_ref=keys.at[source], dst_ref=keys.at[pl.ds((2 * i + 1) * TOK, TOK)],
            send_sem=twin_send.at[i], recv_sem=twin_recv.at[i],
            device_id=(shard + 1 - 2 * core, side), device_id_type=MESH,
        )

    MAP_C, MAP_A, MAP_D, MAP_G, MAP_T = range(5)
    jump = {MAP_C: 1, MAP_A: -1, MAP_D: 1, MAP_G: 2, MAP_T: 1}

    def state_copy(kind, h):
        source = a_ref.at[h] if kind == MAP_A else send_buf.at[kind, h]
        return pltpu.make_async_remote_copy(
            src_ref=source, dst_ref=recv_buf.at[kind, h],
            send_sem=chain_send.at[kind, h], recv_sem=chain_recv.at[kind, h],
            device_id=(ahead(jump[kind]), side), device_id_type=MESH,
        )

    def send_state(kind, h, value=None):
        if value is not None:
            send_buf[kind, h] = value.astype(BF16)
        state_copy(kind, h).start()

    def take_state(kind, h):
        state_copy(kind, h).wait_recv()
        return recv_buf[kind, h]

    sends = {
        MAP_C: is_a,
        MAP_A: is_b,
        MAP_D: is_b & (chip < last),
        MAP_G: is_a & (chip > 0) & (chip < last),
        MAP_T: is_a,
    }
    span = range(heads)

    def emit(h, incoming):
        lanes = slice(h * WIDTH, (h + 1) * WIDTH)
        base[:, lanes] += mul(left_ref[h], incoming)

    loads[0].wait()
    prepare_masks(lens_v[...], shard, pair_mask, link_mask, level_mask, bias)
    pl.semaphore_wait(barrier, expected)
    for i in range(2):
        @pl.when(shard + near[i] < shards)
        def _(i=i):
            near_copy(i).start()
    loads[-1].wait()
    side_start(0)

    for load in loads[1:6]:
        load.wait()
    parts = delta_pairs(heads, (query_v, key_v, value_v, decay_v, beta_v), pair_mask, link_mask)

    for i in range(2):
        @pl.when(shard >= near[i])
        def _(i=i):
            near_copy(i).wait_recv()

        @pl.when(shard < near[i])
        def _(i=i):
            keys[block_rows(SPAN - near[i], side), :] = jnp.zeros((quarter, rank), BF16)

        side_start(i + 1)

    solved = delta_solve(parts, level_mask, a_ref, c_ref)

    @pl.when(is_a)
    def _():
        for h in span:
            send_state(MAP_C, h, c_ref[h])

    @pl.when(is_b)
    def _():
        for h in span:
            send_state(MAP_A, h)

    delta_outputs(parts, solved, left_ref, base)

    @pl.when(is_b)
    def _():
        for h in span:
            incoming = take_state(MAP_C, h)

            @pl.when(chip < last)
            def _():
                send_state(MAP_D, h, c_ref[h] + mul(a_ref[h], incoming))

    @pl.when(is_a)
    def _():
        for h in span:
            step_ref[h] = mul(take_state(MAP_A, h), a_ref[h]).astype(BF16)

    for i in range(SPAN // 2 + 1):
        side_arrived(i)
    for i in range(2):
        twin_copy(i).start()
    for load in loads[6:-1]:
        load.wait()
    for i in range(2):
        twin_copy(i).wait_recv()

    def latent_at(part):
        latent_part(part * 2, 2, scale, latq_v, keys, bias, up_v, mla_v)

    latent_at(0)
    latent_at(1)
    latent_at(2)

    @pl.when(is_a & (chip > 0))
    def _():
        for h in span:
            incoming = take_state(MAP_D, h)

            @pl.when(chip < last)
            def _():
                send_state(MAP_G, h, mul(step_ref[h], incoming))

        for h in span:
            c_ref[h] += mul(a_ref[h], recv_buf[MAP_D, h])
            emit(h, recv_buf[MAP_D, h])

    latent_at(3)

    @pl.when(is_a & (chip <= 1))
    def _():
        for h in span:
            send_state(MAP_T, h, c_ref[h])

    @pl.when(is_a & (chip > 1))
    def _():
        for h in span:
            incoming = take_state(MAP_G, h)
            send_state(MAP_T, h, c_ref[h] + mul(a_ref[h], incoming))
        for h in span:
            emit(h, recv_buf[MAP_G, h])

    @pl.when(is_b)
    def _():
        for h in span:
            emit(h, take_state(MAP_T, h))

    for i in range(2):
        @pl.when(shard + near[i] < shards)
        def _(i=i):
            near_copy(i).wait_send()

        twin_copy(i).wait_send()
    for i in range(SPAN // 2 + 1):
        for step in range(1, head_devices):
            side_copy(i, step, side).wait_send()
    for kind, condition in sends.items():
        @pl.when(condition)
        def _(kind=kind):
            for h in span:
                state_copy(kind, h).wait_send()


def solution(mesh):
    shards = mesh.shape["context"]
    head_devices = mesh.shape["head"]

    def step(query_vec, key_vec, value_vec, log_decay, beta, latent, latent_query, w_uv, doc_lengths):
        rows = query_vec.shape[0]
        heads = beta.shape[1]
        rank = w_uv.shape[0]
        width = query_vec.shape[1]
        keys = (SPAN + 1) * rows
        square = (rows, rows)
        outside = pl.BlockSpec(memory_space=pltpu.HBM)
        inside = pl.BlockSpec(memory_space=pltpu.VMEM)
        dma = pltpu.SemaphoreType.DMA
        side_copies = (SPAN // 2 + 1) * (head_devices - 1)
        return pl.pallas_call(
            functools.partial(body, shards, head_devices, heads, WIDTH**-0.5),
            out_shape=(
                jax.ShapeDtypeStruct((rows, width), F32),
                jax.ShapeDtypeStruct((rows, width), BF16),
            ),
            in_specs=[outside] * 9,
            out_specs=(inside, inside),
            scratch_shapes=[
                pltpu.VMEM((rows, width), F32),
                pltpu.VMEM((rows, width), F32),
                pltpu.VMEM((rows, width), F32),
                pltpu.VMEM((rows, width), F32),
                pltpu.VMEM((heads, rows), F32),
                pltpu.VMEM((rows * heads, rank), BF16),
                pltpu.VMEM((rank, width), BF16),
                pltpu.VMEM((keys, rank), BF16),
                pltpu.VMEM((1, doc_lengths.shape[0]), jnp.int32),
                pltpu.VMEM((2,) + square, F32),
                pltpu.VMEM((2,) + square, F32),
                pltpu.VMEM((LEVELS + 1,) + square, BF16),
                pltpu.VMEM((rows, keys), F32),
                pltpu.VMEM((heads,) + square, BF16),
                pltpu.VMEM((heads,) + square, F32),
                pltpu.VMEM((heads,) + square, BF16),
                pltpu.VMEM((heads,) + square, BF16),
                pltpu.VMEM((5, heads) + square, BF16),
                pltpu.VMEM((5, heads) + square, BF16),
                dma((8 + heads,)),
                dma((5, heads)),
                dma((5, heads)),
                dma((2,)),
                dma((2,)),
                dma((side_copies,)),
                dma((side_copies,)),
                dma((2,)),
                dma((2,)),
            ],
            compiler_params=pltpu.CompilerParams(
                collective_id=0, has_side_effects=True, vmem_limit_bytes=60 * 1024 * 1024
            ),
            cost_estimate=pl.CostEstimate(flops=3_000_000_000, bytes_accessed=6_000_000, transcendentals=1_000_000),
            name="packed_attention",
        )(
            query_vec, key_vec, value_vec, log_decay, beta.T, latent, latent_query, w_uv,
            doc_lengths.reshape(1, -1),
        )

    return jax.shard_map(
        step,
        mesh=mesh,
        in_specs=(
            P("context", "head"),
            P("context", "head"),
            P("context", "head"),
            P("context", "head"),
            P("context", "head"),
            P(("context", "head"), None),
            P("context", "head"),
            P(None, "head"),
            P(),
        ),
        out_specs=(P("context", "head"), P("context", "head")),
        check_vma=False,
    )
```

```python
import functools

import jax
import jax.numpy as jnp
from jax import lax
from jax.experimental import pallas as pl
from jax.experimental.pallas import tpu as pltpu
from jax.sharding import PartitionSpec as P

MESH = pl.DeviceIdType.MESH
F32 = jnp.float32
BF16 = jnp.bfloat16
FAR = -1e30
EPS = 1e-6
SPAN = 4
TOK = 128
WIDTH = 128
LEVELS = 7
BATCH = 4


def mul(left, right):
    return lax.dot_general(left, right, (((1,), (0,)), ((), ())), preferred_element_type=F32)


def mul_nt(left, right):
    return lax.dot_general(left, right, (((1,), (1,)), ((), ())), preferred_element_type=F32)


def mul_tn(left, right):
    return lax.dot_general(left, right, (((0,), (0,)), ((), ())), preferred_element_type=F32)


def halves(matrix):
    high = matrix.astype(BF16)
    return high, (matrix - high.astype(F32)).astype(BF16)


def three(product, left, right):
    return product(left[0], right[0]) + product(left[1], right[0]) + product(left[0], right[1])


def iota2(shape, axis):
    return lax.broadcasted_iota(jnp.int32, shape, axis)


def prepare_masks(lens, shard, pair_mask, link_mask, level_mask, bias):
    square = (TOK, TOK)
    row, col = iota2(square, 0), iota2(square, 1)
    lens_f = lens.astype(F32)
    lens_row = jnp.broadcast_to(lens_f, square)
    begin_col = jnp.sum(jnp.where(col < row, lens_row, 0.0), axis=1, keepdims=True)
    lens_col = jnp.sum(jnp.where(col == row, lens_row, 0.0), axis=1, keepdims=True)
    begin_row = jnp.sum(jnp.where(row < col, lens_col, 0.0), axis=0, keepdims=True)
    low = shard * TOK
    pos_col = (low + iota2((TOK, 1), 0)).astype(F32)
    start_col = jnp.max(jnp.where(begin_row <= pos_col, begin_row, -1.0), axis=1, keepdims=True)
    keys = (SPAN + 1) * TOK
    pos_row = (low - SPAN * TOK + iota2((1, keys), 1)).astype(F32)
    start_row = jnp.max(jnp.where(begin_col <= pos_row, begin_col, -1.0), axis=0, keepdims=True)
    visible = (start_col == start_row) & (pos_row <= pos_col)
    bias[...] = jnp.where(visible, 0.0, FAR)
    same = start_col == start_row[:, SPAN * TOK :]
    pair_mask[0] = jnp.where(same & (row >= col), 1.0, 0.0)
    pair_mask[1] = jnp.where(same & (row > col), 1.0, 0.0)
    link_mask[0] = jnp.broadcast_to(jnp.where(start_col < low.astype(F32), 1.0, 0.0), square)
    link_mask[1] = jnp.broadcast_to(jnp.where(start_col == start_col[TOK - 1 :, :], 1.0, 0.0), square)
    for level in range(LEVELS):
        below = ((row >> (level + 1)) == (col >> (level + 1))) & ((row >> level) > (col >> level))
        level_mask[level] = jnp.where(below, 1.0, 0.0).astype(BF16)
    level_mask[LEVELS] = jnp.where(row == col, 1.0, 0.0).astype(BF16)


def delta_pairs(heads, refs, pair_mask, link_mask):
    query_ref, key_ref, value_ref, decay_ref, beta_ref = refs
    square = (TOK, TOK)
    row, col = iota2(square, 0), iota2(square, 1)
    lower = jnp.where(row >= col, 1.0, 0.0).astype(BF16)
    incl, strict = pair_mask[0] > 0.5, pair_mask[1] > 0.5
    link, tail = link_mask[0], link_mask[1]
    link_last = link[TOK - 1 :, :]
    beta_cols = beta_ref[...].T
    parts = []
    for h in range(heads):
        lanes = slice(h * WIDTH, (h + 1) * WIDTH)
        decay = decay_ref[:, lanes]
        high = decay.astype(BF16)
        rest = decay - high.astype(F32)
        mid = rest.astype(BF16)
        low = (rest - mid.astype(F32)).astype(BF16)
        cum = mul(lower, high) + mul(lower, mid) + mul(lower, low)
        centre, end = cum[TOK // 2 - 1 : TOK // 2, :], cum[TOK - 1 :, :]
        grow, shrink = jnp.exp(cum - centre), jnp.exp(centre - cum)
        from_start, to_end = jnp.exp(centre), jnp.exp(end - centre)
        query, key = query_ref[:, lanes], key_ref[:, lanes]
        query = query * lax.rsqrt(jnp.sum(query * query, axis=1, keepdims=True) + EPS)
        key = key * lax.rsqrt(jnp.sum(key * key, axis=1, keepdims=True) + EPS)
        query_grow, key_grow, key_shrink = query * grow, key * grow, key * shrink
        pairs = three(
            mul_nt, halves(jnp.concatenate([query_grow, key_grow], axis=0)), halves(key_shrink)
        )
        beta = beta_cols[:, h : h + 1]
        in_scale = link * from_start
        parts.append(
            dict(
                weight=halves(jnp.where(incl, pairs[:TOK], 0.0)),
                system=halves(jnp.where(strict, pairs[TOK:], 0.0) * beta),
                query_in=query_grow * in_scale,
                right=jnp.concatenate(
                    [value_ref[:, lanes] * beta, key_grow * in_scale * beta], axis=1
                ),
                tail=halves(key_shrink * (tail * to_end)),
                end=jnp.exp(end) * link_last,
            )
        )
    return parts


def delta_solve(parts, level_mask, a_ref, c_ref):
    square = (TOK, TOK)
    row, col = iota2(square, 0), iota2(square, 1)
    system = [part["system"] for part in parts]
    right = [part["right"] for part in parts]
    span = range(len(parts))
    inverse = [level_mask[LEVELS] - system[h][0] * level_mask[0] for h in span]
    for level in range(1, LEVELS):
        inner = [mul(system[h][0] * level_mask[level], inverse[h]).astype(BF16) for h in span]
        inverse = [inverse[h] - mul(inverse[h], inner[h]).astype(BF16) for h in span]
    solved = [mul(inverse[h], right[h].astype(BF16)) for h in span]
    rest = [right[h] - solved[h] - three(mul, system[h], halves(solved[h])) for h in span]
    solved = [halves(solved[h] + mul(inverse[h], rest[h].astype(BF16))) for h in span]
    for h in span:
        change = three(mul_tn, parts[h]["tail"], solved[h])
        c_ref[h] = change[:, :WIDTH]
        a_ref[h] = (jnp.where(row == col, parts[h]["end"], 0.0) - change[:, WIDTH:]).astype(BF16)
    return solved


def delta_outputs(parts, solved, left_ref, base_ref):
    for h in range(len(parts)):
        output = three(mul, parts[h]["weight"], solved[h])
        base_ref[:, h * WIDTH : (h + 1) * WIDTH] = output[:, :WIDTH]
        left_ref[h] = (parts[h]["query_in"] - output[:, WIDTH:]).astype(BF16)


def latent_part(first, heads, scale, query_rows, keys, bias, up_ref, out_ref):
    rows = heads * TOK
    scores = mul_nt(query_rows[first * TOK : first * TOK + rows, :], keys[...])
    mask = jnp.concatenate([bias[...]] * heads, axis=0)
    scores = scores * scale + mask
    top = jnp.max(scores, axis=1, keepdims=True)
    weights = jnp.exp(scores - top)
    totals = jnp.sum(weights, axis=1, keepdims=True)
    context = mul(weights.astype(BF16), keys[...]) * (1.0 / totals)
    context = context.astype(BF16)
    for h in range(heads):
        at = (first + h) * WIDTH
        out_ref[:, at : at + WIDTH] = mul(
            context[h * TOK : (h + 1) * TOK], up_ref[:, at : at + WIDTH]
        ).astype(BF16)


def body(
    shards, head_devices, heads, scale,
    query_hbm, key_hbm, value_hbm, decay_hbm, beta_hbm, latent_hbm, latq_hbm, up_hbm, lens_hbm,
    base, mla_v,
    query_v, key_v, value_v, decay_v, beta_v, latq_v, up_v, keys, lens_v,
    pair_mask, link_mask, level_mask, bias,
    a_ref, c_ref, left_ref, step_ref, send_buf, recv_buf,
    load_sem, chain_send, chain_recv, near_send, near_recv, side_send, side_recv, twin_send, twin_recv,
):
    shard = lax.axis_index("context")
    side = lax.axis_index("head")
    core = lax.rem(shard, 2)
    chip = shard // 2
    last = shards // 2 - 1
    is_a, is_b = core == 0, core == 1
    rank = latq_v.shape[1]
    quarter = TOK // head_devices
    near = (2, 4)
    batch = BATCH

    def ahead(steps):
        return lax.rem(shard + shards + steps, shards)

    def block_rows(block, place):
        return pl.ds(pl.multiple_of(block * TOK + place * quarter, quarter), quarter)

    pairs = [(lens_hbm, lens_v), (decay_hbm, decay_v), (key_hbm, key_v), (query_hbm, query_v)]
    pairs += [(value_hbm, value_v), (beta_hbm, beta_v), (up_hbm, up_v)]
    pairs += [
        (latq_hbm.at[:, pl.ds(h * rank, rank)], latq_v.at[pl.ds(h * TOK, TOK), :]) for h in range(heads)
    ]
    pairs += [(latent_hbm, keys.at[block_rows(SPAN, side)])]
    loads = [pltpu.make_async_copy(pairs[i][0], pairs[i][1], load_sem.at[i]) for i in range(len(pairs))]
    loads[0].start()
    loads[-1].start()
    for load in loads[1:-1]:
        load.start()

    barrier = pltpu.get_barrier_semaphore()

    def greet(peer):
        pl.semaphore_signal(barrier, inc=1, device_id=peer, device_id_type=MESH)

    for step in range(1, head_devices):
        greet((shard, lax.rem(side + step, head_devices)))
    for steps in (1,) + near:
        @pl.when(shard >= steps)
        def _(steps=steps):
            greet((ahead(-steps), side))

    @pl.when(is_a)
    def _():
        greet((ahead(1), side))

    def one_if(condition):
        return jnp.where(condition, 1, 0).astype(jnp.int32)

    expected = head_devices - 1 + core
    for steps in (1,) + near:
        expected = expected + one_if(shard + steps < shards)

    def near_copy(i):
        return pltpu.make_async_remote_copy(
            src_ref=latent_hbm, dst_ref=keys.at[block_rows(SPAN - near[i], side)],
            send_sem=near_send.at[i], recv_sem=near_recv.at[i],
            device_id=(ahead(near[i]), side), device_id_type=MESH,
        )

    def side_copy(i, step, place):
        rows = block_rows(SPAN - 2 * i, place)
        at = i * (head_devices - 1) + step - 1
        return pltpu.make_async_remote_copy(
            src_ref=keys.at[rows], dst_ref=keys.at[rows],
            send_sem=side_send.at[at], recv_sem=side_recv.at[at],
            device_id=(shard, lax.rem(side + step, head_devices)), device_id_type=MESH,
        )

    def side_start(i):
        for step in range(1, head_devices):
            side_copy(i, step, side).start()

    def side_arrived(i):
        for step in range(1, head_devices):
            side_copy(i, step, lax.rem(side + head_devices - step, head_devices)).wait_recv()

    def twin_copy(i):
        source = pl.ds(pl.multiple_of((2 * i + 2 * (1 - core)) * TOK, TOK), TOK)
        return pltpu.make_async_remote_copy(
            src_ref=keys.at[source], dst_ref=keys.at[pl.ds((2 * i + 1) * TOK, TOK)],
            send_sem=twin_send.at[i], recv_sem=twin_recv.at[i],
            device_id=(shard + 1 - 2 * core, side), device_id_type=MESH,
        )

    MAP_C, MAP_A, MAP_D, MAP_G, MAP_T = range(5)
    jump = {MAP_C: 1, MAP_A: -1, MAP_D: 1, MAP_G: 2, MAP_T: 1}

    def state_copy(kind, group):
        part = pl.ds(group * batch, batch)
        source = a_ref.at[part] if kind == MAP_A else send_buf.at[kind, part]
        return pltpu.make_async_remote_copy(
            src_ref=source, dst_ref=recv_buf.at[kind, part],
            send_sem=chain_send.at[kind, group], recv_sem=chain_recv.at[kind, group],
            device_id=(ahead(jump[kind]), side), device_id_type=MESH,
        )

    def members(group):
        return range(group * batch, (group + 1) * batch)

    def send_state(kind, group, values=None):
        if values is not None:
            for h, value in zip(members(group), values):
                send_buf[kind, h] = value.astype(BF16)
        state_copy(kind, group).start()

    def take_state(kind, group):
        state_copy(kind, group).wait_recv()
        return [recv_buf[kind, h] for h in members(group)]

    sends = {
        MAP_C: is_a,
        MAP_A: is_b,
        MAP_D: is_b & (chip < last),
        MAP_G: is_a & (chip > 0) & (chip < last),
        MAP_T: is_a,
    }
    groups = range(heads // batch)

    def emit(group, incoming):
        for h, state in zip(members(group), incoming):
            lanes = slice(h * WIDTH, (h + 1) * WIDTH)
            base[:, lanes] += mul(left_ref[h], state)

    loads[0].wait()
    prepare_masks(lens_v[...], shard, pair_mask, link_mask, level_mask, bias)
    pl.semaphore_wait(barrier, expected)
    for i in range(2):
        @pl.when(shard + near[i] < shards)
        def _(i=i):
            near_copy(i).start()
    loads[-1].wait()
    side_start(0)

    for load in loads[1:6]:
        load.wait()
    parts = delta_pairs(heads, (query_v, key_v, value_v, decay_v, beta_v), pair_mask, link_mask)

    solved = delta_solve(parts, level_mask, a_ref, c_ref)

    @pl.when(is_a)
    def _():
        for group in groups:
            send_state(MAP_C, group, [c_ref[h] for h in members(group)])

    @pl.when(is_b)
    def _():
        for group in groups:
            send_state(MAP_A, group)

    for i in range(2):
        @pl.when(shard >= near[i])
        def _(i=i):
            near_copy(i).wait_recv()

        @pl.when(shard < near[i])
        def _(i=i):
            keys[block_rows(SPAN - near[i], side), :] = jnp.zeros((quarter, rank), BF16)

        side_start(i + 1)

    delta_outputs(parts, solved, left_ref, base)

    @pl.when(is_b & (chip < last))
    def _():
        for group in groups:
            incoming = take_state(MAP_C, group)
            send_state(
                MAP_D, group, [c_ref[h] + mul(a_ref[h], x) for h, x in zip(members(group), incoming)]
            )

    @pl.when(is_b & (chip == last))
    def _():
        for group in groups:
            take_state(MAP_C, group)

    @pl.when(is_a)
    def _():
        for group in groups:
            incoming = take_state(MAP_A, group)
            for h, x in zip(members(group), incoming):
                step_ref[h] = mul(x, a_ref[h]).astype(BF16)

    for i in range(SPAN // 2 + 1):
        side_arrived(i)
    for i in range(2):
        twin_copy(i).start()

    @pl.when(is_a & (chip > 0) & (chip < last))
    def _():
        for group in groups:
            incoming = take_state(MAP_D, group)
            send_state(MAP_G, group, [mul(step_ref[h], x) for h, x in zip(members(group), incoming)])

    @pl.when(is_a & (chip == last))
    def _():
        for group in groups:
            take_state(MAP_D, group)

    for load in loads[6:-1]:
        load.wait()
    for i in range(2):
        twin_copy(i).wait_recv()

    def latent_at(part):
        latent_part(part * 4, 4, scale, latq_v, keys, bias, up_v, mla_v)

    latent_at(0)

    latent_at(1)

    @pl.when(is_a & (chip > 0))
    def _():
        for group in groups:
            for h in members(group):
                c_ref[h] += mul(a_ref[h], recv_buf[MAP_D, h])
            emit(group, [recv_buf[MAP_D, h] for h in members(group)])

    @pl.when(is_a & (chip <= 1))
    def _():
        for group in groups:
            send_state(MAP_T, group, [c_ref[h] for h in members(group)])

    @pl.when(is_a & (chip > 1))
    def _():
        for group in groups:
            incoming = take_state(MAP_G, group)
            send_state(
                MAP_T, group, [c_ref[h] + mul(a_ref[h], x) for h, x in zip(members(group), incoming)]
            )
        for group in groups:
            emit(group, [recv_buf[MAP_G, h] for h in members(group)])

    @pl.when(is_b)
    def _():
        for group in groups:
            emit(group, take_state(MAP_T, group))

    for i in range(2):
        @pl.when(shard + near[i] < shards)
        def _(i=i):
            near_copy(i).wait_send()

        twin_copy(i).wait_send()
    for i in range(SPAN // 2 + 1):
        for step in range(1, head_devices):
            side_copy(i, step, side).wait_send()
    for kind, condition in sends.items():
        @pl.when(condition)
        def _(kind=kind):
            for group in groups:
                state_copy(kind, group).wait_send()


def solution(mesh):
    shards = mesh.shape["context"]
    head_devices = mesh.shape["head"]

    def step(query_vec, key_vec, value_vec, log_decay, beta, latent, latent_query, w_uv, doc_lengths):
        rows = query_vec.shape[0]
        heads = beta.shape[1]
        rank = w_uv.shape[0]
        width = query_vec.shape[1]
        keys = (SPAN + 1) * rows
        square = (rows, rows)
        outside = pl.BlockSpec(memory_space=pltpu.HBM)
        inside = pl.BlockSpec(memory_space=pltpu.VMEM)
        dma = pltpu.SemaphoreType.DMA
        side_copies = (SPAN // 2 + 1) * (head_devices - 1)
        inputs = (query_vec, key_vec, value_vec, log_decay, beta.T, latent, latent_query, w_uv, doc_lengths.reshape(1, -1))
        inputs = [pltpu.with_memory_space_constraint(x, pltpu.HBM) for x in inputs]
        return pl.pallas_call(
            functools.partial(body, shards, head_devices, heads, WIDTH**-0.5),
            out_shape=(
                jax.ShapeDtypeStruct((rows, width), F32),
                jax.ShapeDtypeStruct((rows, width), BF16),
            ),
            in_specs=[outside] * 9,
            out_specs=(inside, inside),
            scratch_shapes=[
                pltpu.VMEM((rows, width), F32),
                pltpu.VMEM((rows, width), F32),
                pltpu.VMEM((rows, width), F32),
                pltpu.VMEM((rows, width), F32),
                pltpu.VMEM((heads, rows), F32),
                pltpu.VMEM((rows * heads, rank), BF16),
                pltpu.VMEM((rank, width), BF16),
                pltpu.VMEM((keys, rank), BF16),
                pltpu.VMEM((1, doc_lengths.shape[0]), jnp.int32),
                pltpu.VMEM((2,) + square, F32),
                pltpu.VMEM((2,) + square, F32),
                pltpu.VMEM((LEVELS + 1,) + square, BF16),
                pltpu.VMEM((rows, keys), F32),
                pltpu.VMEM((heads,) + square, BF16),
                pltpu.VMEM((heads,) + square, F32),
                pltpu.VMEM((heads,) + square, BF16),
                pltpu.VMEM((heads,) + square, BF16),
                pltpu.VMEM((5, heads) + square, BF16),
                pltpu.VMEM((5, heads) + square, BF16),
                dma((8 + heads,)),
                dma((5, heads // BATCH)),
                dma((5, heads // BATCH)),
                dma((2,)),
                dma((2,)),
                dma((side_copies,)),
                dma((side_copies,)),
                dma((2,)),
                dma((2,)),
            ],
            compiler_params=pltpu.CompilerParams(
                collective_id=0, has_side_effects=True, vmem_limit_bytes=48 * 1024 * 1024
            ),
            cost_estimate=pl.CostEstimate(flops=3_000_000_000, bytes_accessed=6_000_000, transcendentals=1_000_000),
            name="packed_attention",
        )(*inputs)

    return jax.shard_map(
        step,
        mesh=mesh,
        in_specs=(
            P("context", "head"),
            P("context", "head"),
            P("context", "head"),
            P("context", "head"),
            P("context", "head"),
            P(("context", "head"), None),
            P("context", "head"),
            P(None, "head"),
            P(),
        ),
        out_specs=(P("context", "head"), P("context", "head")),
        check_vma=False,
    )
```

```python
import functools

import jax
import jax.numpy as jnp
from jax import lax
from jax.experimental import pallas as pl
from jax.experimental.pallas import tpu as pltpu
from jax.sharding import PartitionSpec as P

MESH = pl.DeviceIdType.MESH
F32 = jnp.float32
BF16 = jnp.bfloat16
FAR = -1e30
EPS = 1e-6
SPAN = 4
TOK = 128
WIDTH = 128
LEVELS = 7
BATCH = 4


def mul(left, right):
    return lax.dot_general(left, right, (((1,), (0,)), ((), ())), preferred_element_type=F32)


def mul_nt(left, right):
    return lax.dot_general(left, right, (((1,), (1,)), ((), ())), preferred_element_type=F32)


def mul_tn(left, right):
    return lax.dot_general(left, right, (((0,), (0,)), ((), ())), preferred_element_type=F32)


def halves(matrix):
    high = matrix.astype(BF16)
    return high, (matrix - high.astype(F32)).astype(BF16)


def three(product, left, right):
    return product(left[0], right[0]) + product(left[1], right[0]) + product(left[0], right[1])


def iota2(shape, axis):
    return lax.broadcasted_iota(jnp.int32, shape, axis)


def prepare_masks(lens, shard, pair_mask, link_mask, level_mask, bias):
    square = (TOK, TOK)
    row, col = iota2(square, 0), iota2(square, 1)
    lens_f = lens.astype(F32)
    lens_row = jnp.broadcast_to(lens_f, square)
    begin_col = jnp.sum(jnp.where(col < row, lens_row, 0.0), axis=1, keepdims=True)
    lens_col = jnp.sum(jnp.where(col == row, lens_row, 0.0), axis=1, keepdims=True)
    begin_row = jnp.sum(jnp.where(row < col, lens_col, 0.0), axis=0, keepdims=True)
    low = shard * TOK
    pos_col = (low + iota2((TOK, 1), 0)).astype(F32)
    start_col = jnp.max(jnp.where(begin_row <= pos_col, begin_row, -1.0), axis=1, keepdims=True)
    keys = (SPAN + 1) * TOK
    pos_row = (low - SPAN * TOK + iota2((1, keys), 1)).astype(F32)
    start_row = jnp.max(jnp.where(begin_col <= pos_row, begin_col, -1.0), axis=0, keepdims=True)
    visible = (start_col == start_row) & (pos_row <= pos_col)
    bias[...] = jnp.where(visible, 0.0, FAR)
    same = start_col == start_row[:, SPAN * TOK :]
    pair_mask[0] = jnp.where(same & (row >= col), 1.0, 0.0)
    pair_mask[1] = jnp.where(same & (row > col), 1.0, 0.0)
    link_mask[0] = jnp.broadcast_to(jnp.where(start_col < low.astype(F32), 1.0, 0.0), square)
    link_mask[1] = jnp.broadcast_to(jnp.where(start_col == start_col[TOK - 1 :, :], 1.0, 0.0), square)
    for level in range(LEVELS):
        below = ((row >> (level + 1)) == (col >> (level + 1))) & ((row >> level) > (col >> level))
        level_mask[level] = jnp.where(below, 1.0, 0.0).astype(BF16)
    level_mask[LEVELS] = jnp.where(row == col, 1.0, 0.0).astype(BF16)


def delta_pairs(heads, refs, pair_mask, link_mask):
    query_ref, key_ref, value_ref, decay_ref, beta_ref = refs
    square = (TOK, TOK)
    row, col = iota2(square, 0), iota2(square, 1)
    lower = jnp.where(row >= col, 1.0, 0.0).astype(BF16)
    incl, strict = pair_mask[0] > 0.5, pair_mask[1] > 0.5
    link, tail = link_mask[0], link_mask[1]
    link_last = link[TOK - 1 :, :]
    beta_cols = beta_ref[...].T
    parts = []
    for h in range(heads):
        lanes = slice(h * WIDTH, (h + 1) * WIDTH)
        decay = decay_ref[:, lanes]
        high = decay.astype(BF16)
        rest = decay - high.astype(F32)
        mid = rest.astype(BF16)
        low = (rest - mid.astype(F32)).astype(BF16)
        cum = mul(lower, high) + mul(lower, mid) + mul(lower, low)
        centre, end = cum[TOK // 2 - 1 : TOK // 2, :], cum[TOK - 1 :, :]
        grow, shrink = jnp.exp(cum - centre), jnp.exp(centre - cum)
        from_start, to_end = jnp.exp(centre), jnp.exp(end - centre)
        query, key = query_ref[:, lanes], key_ref[:, lanes]
        query = query * lax.rsqrt(jnp.sum(query * query, axis=1, keepdims=True) + EPS)
        key = key * lax.rsqrt(jnp.sum(key * key, axis=1, keepdims=True) + EPS)
        query_grow, key_grow, key_shrink = query * grow, key * grow, key * shrink
        pairs = three(
            mul_nt, halves(jnp.concatenate([query_grow, key_grow], axis=0)), halves(key_shrink)
        )
        beta = beta_cols[:, h : h + 1]
        in_scale = link * from_start
        parts.append(
            dict(
                weight=halves(jnp.where(incl, pairs[:TOK], 0.0)),
                system=halves(jnp.where(strict, pairs[TOK:], 0.0) * beta),
                query_in=query_grow * in_scale,
                right=jnp.concatenate(
                    [value_ref[:, lanes] * beta, key_grow * in_scale * beta], axis=1
                ),
                tail=halves(key_shrink * (tail * to_end)),
                end=jnp.exp(end) * link_last,
            )
        )
    return parts


def delta_solve(parts, level_mask, a_ref, c_ref, midway, finished):
    square = (TOK, TOK)
    row, col = iota2(square, 0), iota2(square, 1)
    system = [part["system"] for part in parts]
    right = [part["right"] for part in parts]
    span = range(len(parts))
    inverse = [level_mask[LEVELS] - system[h][0] * level_mask[0] for h in span]
    for level in range(1, LEVELS):
        if level == LEVELS // 2:
            midway()
        inner = [mul(system[h][0] * level_mask[level], inverse[h]).astype(BF16) for h in span]
        inverse = [inverse[h] - mul(inverse[h], inner[h]).astype(BF16) for h in span]
    solved = [mul(inverse[h], right[h].astype(BF16)) for h in span]
    rest = [right[h] - solved[h] - three(mul, system[h], halves(solved[h])) for h in span]
    solved = [halves(solved[h] + mul(inverse[h], rest[h].astype(BF16))) for h in span]
    for group in range(len(parts) // BATCH):
        for h in range(group * BATCH, (group + 1) * BATCH):
            change = three(mul_tn, parts[h]["tail"], solved[h])
            c_ref[h] = change[:, :WIDTH]
            a_ref[h] = (jnp.where(row == col, parts[h]["end"], 0.0) - change[:, WIDTH:]).astype(BF16)
        finished(group)
    return solved


def delta_outputs(parts, solved, left_ref, base_ref):
    for h in range(len(parts)):
        output = three(mul, parts[h]["weight"], solved[h])
        base_ref[:, h * WIDTH : (h + 1) * WIDTH] = output[:, :WIDTH]
        left_ref[h] = (parts[h]["query_in"] - output[:, WIDTH:]).astype(BF16)


def latent_part(first, heads, scale, query_rows, keys, bias, up_ref, out_ref):
    rows = heads * TOK
    scores = mul_nt(query_rows[first * TOK : first * TOK + rows, :], keys[...])
    mask = jnp.concatenate([bias[...]] * heads, axis=0)
    scores = scores * scale + mask
    top = jnp.max(scores, axis=1, keepdims=True)
    weights = jnp.exp(scores - top)
    totals = jnp.sum(weights, axis=1, keepdims=True)
    context = mul(weights.astype(BF16), keys[...]) * (1.0 / totals)
    context = context.astype(BF16)
    for h in range(heads):
        at = (first + h) * WIDTH
        out_ref[:, at : at + WIDTH] = mul(
            context[h * TOK : (h + 1) * TOK], up_ref[:, at : at + WIDTH]
        ).astype(BF16)


def body(
    shards, head_devices, heads, scale,
    query_hbm, key_hbm, value_hbm, decay_hbm, beta_hbm, latent_hbm, latq_hbm, up_hbm, lens_hbm,
    base, mla_v,
    query_v, key_v, value_v, decay_v, beta_v, latq_v, up_v, keys, lens_v,
    pair_mask, link_mask, level_mask, bias,
    a_ref, c_ref, left_ref, step_ref, send_buf, recv_buf,
    load_sem, chain_send, chain_recv, near_send, near_recv, side_send, side_recv, twin_send, twin_recv,
):
    shard = lax.axis_index("context")
    side = lax.axis_index("head")
    core = lax.rem(shard, 2)
    chip = shard // 2
    last = shards // 2 - 1
    is_a, is_b = core == 0, core == 1
    rank = latq_v.shape[1]
    quarter = TOK // head_devices
    near = (2, 4)
    batch = BATCH

    def ahead(steps):
        return lax.rem(shard + shards + steps, shards)

    def block_rows(block, place):
        return pl.ds(pl.multiple_of(block * TOK + place * quarter, quarter), quarter)

    pairs = [(lens_hbm, lens_v), (decay_hbm, decay_v), (key_hbm, key_v), (query_hbm, query_v)]
    pairs += [(value_hbm, value_v), (beta_hbm, beta_v), (up_hbm, up_v)]
    pairs += [
        (latq_hbm.at[:, pl.ds(h * rank, rank)], latq_v.at[pl.ds(h * TOK, TOK), :]) for h in range(heads)
    ]
    pairs += [(latent_hbm, keys.at[block_rows(SPAN, side)])]
    loads = [pltpu.make_async_copy(pairs[i][0], pairs[i][1], load_sem.at[i]) for i in range(len(pairs))]
    loads[0].start()
    loads[-1].start()
    for load in loads[1:-1]:
        load.start()

    barrier = pltpu.get_barrier_semaphore()

    def greet(peer):
        pl.semaphore_signal(barrier, inc=1, device_id=peer, device_id_type=MESH)

    for step in range(1, head_devices):
        greet((shard, lax.rem(side + step, head_devices)))
    for steps in (1,) + near:
        @pl.when(shard >= steps)
        def _(steps=steps):
            greet((ahead(-steps), side))

    @pl.when(is_a)
    def _():
        greet((ahead(1), side))

    def one_if(condition):
        return jnp.where(condition, 1, 0).astype(jnp.int32)

    expected = head_devices - 1 + core
    for steps in (1,) + near:
        expected = expected + one_if(shard + steps < shards)

    def near_copy(i):
        return pltpu.make_async_remote_copy(
            src_ref=latent_hbm, dst_ref=keys.at[block_rows(SPAN - near[i], side)],
            send_sem=near_send.at[i], recv_sem=near_recv.at[i],
            device_id=(ahead(near[i]), side), device_id_type=MESH,
        )

    def side_copy(i, step, place):
        rows = block_rows(SPAN - 2 * i, place)
        at = i * (head_devices - 1) + step - 1
        return pltpu.make_async_remote_copy(
            src_ref=keys.at[rows], dst_ref=keys.at[rows],
            send_sem=side_send.at[at], recv_sem=side_recv.at[at],
            device_id=(shard, lax.rem(side + step, head_devices)), device_id_type=MESH,
        )

    def side_start(i):
        for step in range(1, head_devices):
            side_copy(i, step, side).start()

    def side_arrived(i):
        for step in range(1, head_devices):
            side_copy(i, step, lax.rem(side + head_devices - step, head_devices)).wait_recv()

    def twin_copy(i):
        source = pl.ds(pl.multiple_of((2 * i + 2 * (1 - core)) * TOK, TOK), TOK)
        return pltpu.make_async_remote_copy(
            src_ref=keys.at[source], dst_ref=keys.at[pl.ds((2 * i + 1) * TOK, TOK)],
            send_sem=twin_send.at[i], recv_sem=twin_recv.at[i],
            device_id=(shard + 1 - 2 * core, side), device_id_type=MESH,
        )

    MAP_C, MAP_A, MAP_D, MAP_G, MAP_T = range(5)
    jump = {MAP_C: 1, MAP_A: -1, MAP_D: 1, MAP_G: 2, MAP_T: 1}

    def state_copy(kind, group):
        part = pl.ds(group * batch, batch)
        source = a_ref.at[part] if kind == MAP_A else send_buf.at[kind, part]
        return pltpu.make_async_remote_copy(
            src_ref=source, dst_ref=recv_buf.at[kind, part],
            send_sem=chain_send.at[kind, group], recv_sem=chain_recv.at[kind, group],
            device_id=(ahead(jump[kind]), side), device_id_type=MESH,
        )

    def members(group):
        return range(group * batch, (group + 1) * batch)

    def send_state(kind, group, values=None):
        if values is not None:
            for h, value in zip(members(group), values):
                send_buf[kind, h] = value.astype(BF16)
        state_copy(kind, group).start()

    def take_state(kind, group):
        state_copy(kind, group).wait_recv()
        return [recv_buf[kind, h] for h in members(group)]

    sends = {
        MAP_C: is_a,
        MAP_A: is_b,
        MAP_D: is_b & (chip < last),
        MAP_G: is_a & (chip > 0) & (chip < last),
        MAP_T: is_a,
    }
    groups = range(heads // batch)

    def emit(group, incoming):
        for h, state in zip(members(group), incoming):
            lanes = slice(h * WIDTH, (h + 1) * WIDTH)
            base[:, lanes] += mul(left_ref[h], state)

    loads[0].wait()
    prepare_masks(lens_v[...], shard, pair_mask, link_mask, level_mask, bias)
    for load in loads[1:6]:
        load.wait()
    parts = delta_pairs(heads, (query_v, key_v, value_v, decay_v, beta_v), pair_mask, link_mask)

    def open_links():
        pl.semaphore_wait(barrier, expected)
        for i in range(2):
            @pl.when(shard + near[i] < shards)
            def _(i=i):
                near_copy(i).start()
        loads[-1].wait()
        side_start(0)

    def send_maps(group):
        @pl.when(is_a)
        def _():
            send_state(MAP_C, group, [c_ref[h] for h in members(group)])

        @pl.when(is_b)
        def _():
            send_state(MAP_A, group)

    solved = delta_solve(parts, level_mask, a_ref, c_ref, open_links, send_maps)

    delta_outputs(parts, solved, left_ref, base)

    @pl.when(is_b & (chip < last))
    def _():
        for group in groups:
            incoming = take_state(MAP_C, group)
            send_state(
                MAP_D, group, [c_ref[h] + mul(a_ref[h], x) for h, x in zip(members(group), incoming)]
            )

    @pl.when(is_b & (chip == last))
    def _():
        for group in groups:
            take_state(MAP_C, group)

    @pl.when(is_a)
    def _():
        for group in groups:
            incoming = take_state(MAP_A, group)
            for h, x in zip(members(group), incoming):
                step_ref[h] = mul(x, a_ref[h]).astype(BF16)

    for i in range(2):
        @pl.when(shard >= near[i])
        def _(i=i):
            near_copy(i).wait_recv()

        @pl.when(shard < near[i])
        def _(i=i):
            keys[block_rows(SPAN - near[i], side), :] = jnp.zeros((quarter, rank), BF16)

        side_start(i + 1)

    @pl.when(is_a & (chip > 0) & (chip < last))
    def _():
        for group in groups:
            incoming = take_state(MAP_D, group)
            send_state(MAP_G, group, [mul(step_ref[h], x) for h, x in zip(members(group), incoming)])

    @pl.when(is_a & (chip == last))
    def _():
        for group in groups:
            take_state(MAP_D, group)

    side_arrived(0)

    @pl.when(is_a)
    def _():
        twin_copy(1).start()

    side_arrived(1)

    @pl.when(is_a)
    def _():
        twin_copy(0).start()

    @pl.when(is_b)
    def _():
        twin_copy(1).start()

    side_arrived(2)

    @pl.when(is_b)
    def _():
        twin_copy(0).start()

    for load in loads[6:-1]:
        load.wait()
    for i in range(2):
        twin_copy(i).wait_recv()

    def latent_at(part):
        latent_part(part * 4, 4, scale, latq_v, keys, bias, up_v, mla_v)

    latent_at(0)

    @pl.when(is_a & (chip <= 1))
    def _():
        @pl.when(chip == 1)
        def _():
            for group in groups:
                for h in members(group):
                    c_ref[h] += mul(a_ref[h], recv_buf[MAP_D, h])

        for group in groups:
            send_state(MAP_T, group, [c_ref[h] for h in members(group)])

    @pl.when(is_a & (chip > 1))
    def _():
        for h in range(heads):
            c_ref[h] += mul(a_ref[h], recv_buf[MAP_D, h])
        for group in groups:
            incoming = take_state(MAP_G, group)
            send_state(
                MAP_T, group, [c_ref[h] + mul(a_ref[h], x) for h, x in zip(members(group), incoming)]
            )

    latent_at(1)

    @pl.when(is_a & (chip == 1))
    def _():
        for group in groups:
            emit(group, [recv_buf[MAP_D, h] for h in members(group)])

    @pl.when(is_a & (chip > 1))
    def _():
        for group in groups:
            for h in members(group):
                lanes = slice(h * WIDTH, (h + 1) * WIDTH)
                base[:, lanes] += mul(left_ref[h], recv_buf[MAP_D, h]) + mul(left_ref[h], recv_buf[MAP_G, h])

    @pl.when(is_b)
    def _():
        for group in groups:
            emit(group, take_state(MAP_T, group))

    for i in range(2):
        @pl.when(shard + near[i] < shards)
        def _(i=i):
            near_copy(i).wait_send()

        twin_copy(i).wait_send()
    for i in range(SPAN // 2 + 1):
        for step in range(1, head_devices):
            side_copy(i, step, side).wait_send()
    for kind, condition in sends.items():
        @pl.when(condition)
        def _(kind=kind):
            for group in groups:
                state_copy(kind, group).wait_send()


def solution(mesh):
    shards = mesh.shape["context"]
    head_devices = mesh.shape["head"]

    def step(query_vec, key_vec, value_vec, log_decay, beta, latent, latent_query, w_uv, doc_lengths):
        rows = query_vec.shape[0]
        heads = beta.shape[1]
        rank = w_uv.shape[0]
        width = query_vec.shape[1]
        keys = (SPAN + 1) * rows
        square = (rows, rows)
        outside = pl.BlockSpec(memory_space=pltpu.HBM)
        inside = pl.BlockSpec(memory_space=pltpu.VMEM)
        dma = pltpu.SemaphoreType.DMA
        side_copies = (SPAN // 2 + 1) * (head_devices - 1)
        inputs = (query_vec, key_vec, value_vec, log_decay, beta.T, latent, latent_query, w_uv, doc_lengths.reshape(1, -1))
        inputs = [pltpu.with_memory_space_constraint(x, pltpu.HBM) for x in inputs]
        return pl.pallas_call(
            functools.partial(body, shards, head_devices, heads, WIDTH**-0.5),
            out_shape=(
                jax.ShapeDtypeStruct((rows, width), F32),
                jax.ShapeDtypeStruct((rows, width), BF16),
            ),
            in_specs=[outside] * 9,
            out_specs=(inside, inside),
            scratch_shapes=[
                pltpu.VMEM((rows, width), F32),
                pltpu.VMEM((rows, width), F32),
                pltpu.VMEM((rows, width), F32),
                pltpu.VMEM((rows, width), F32),
                pltpu.VMEM((heads, rows), F32),
                pltpu.VMEM((rows * heads, rank), BF16),
                pltpu.VMEM((rank, width), BF16),
                pltpu.VMEM((keys, rank), BF16),
                pltpu.VMEM((1, doc_lengths.shape[0]), jnp.int32),
                pltpu.VMEM((2,) + square, F32),
                pltpu.VMEM((2,) + square, F32),
                pltpu.VMEM((LEVELS + 1,) + square, BF16),
                pltpu.VMEM((rows, keys), F32),
                pltpu.VMEM((heads,) + square, BF16),
                pltpu.VMEM((heads,) + square, F32),
                pltpu.VMEM((heads,) + square, BF16),
                pltpu.VMEM((heads,) + square, BF16),
                pltpu.VMEM((5, heads) + square, BF16),
                pltpu.VMEM((5, heads) + square, BF16),
                dma((8 + heads,)),
                dma((5, heads // BATCH)),
                dma((5, heads // BATCH)),
                dma((2,)),
                dma((2,)),
                dma((side_copies,)),
                dma((side_copies,)),
                dma((2,)),
                dma((2,)),
            ],
            compiler_params=pltpu.CompilerParams(
                collective_id=0, has_side_effects=True, vmem_limit_bytes=48 * 1024 * 1024
            ),
            cost_estimate=pl.CostEstimate(flops=3_000_000_000, bytes_accessed=6_000_000, transcendentals=1_000_000),
            name="packed_attention",
        )(*inputs)

    return jax.shard_map(
        step,
        mesh=mesh,
        in_specs=(
            P("context", "head"),
            P("context", "head"),
            P("context", "head"),
            P("context", "head"),
            P("context", "head"),
            P(("context", "head"), None),
            P("context", "head"),
            P(None, "head"),
            P(),
        ),
        out_specs=(P("context", "head"), P("context", "head")),
        check_vma=False,
    )
```

```python
import functools

import jax
import jax.numpy as jnp
from jax import lax
from jax.experimental import pallas as pl
from jax.experimental.pallas import tpu as pltpu
from jax.sharding import PartitionSpec as P

MESH = pl.DeviceIdType.MESH
F32 = jnp.float32
BF16 = jnp.bfloat16
FAR = -1e30
EPS = 1e-6
SPAN = 4
TOK = 128
WIDTH = 128
LEVELS = 7
BATCH = 4
PIECES = 2


def mul(left, right):
    return lax.dot_general(left, right, (((1,), (0,)), ((), ())), preferred_element_type=F32)


def mul_nt(left, right):
    return lax.dot_general(left, right, (((1,), (1,)), ((), ())), preferred_element_type=F32)


def mul_tn(left, right):
    return lax.dot_general(left, right, (((0,), (0,)), ((), ())), preferred_element_type=F32)


def halves(matrix):
    high = matrix.astype(BF16)
    return high, (matrix - high.astype(F32)).astype(BF16)


def three(product, left, right):
    return product(left[0], right[0]) + product(left[1], right[0]) + product(left[0], right[1])


def iota2(shape, axis):
    return lax.broadcasted_iota(jnp.int32, shape, axis)


def prepare_masks(lens, shard, pair_mask, link_mask, level_mask):
    square = (TOK, TOK)
    row, col = iota2(square, 0), iota2(square, 1)
    lens_f = lens.astype(F32)
    lens_row = jnp.broadcast_to(lens_f, square)
    begin_col = jnp.sum(jnp.where(col < row, lens_row, 0.0), axis=1, keepdims=True)
    lens_col = jnp.sum(jnp.where(col == row, lens_row, 0.0), axis=1, keepdims=True)
    begin_row = jnp.sum(jnp.where(row < col, lens_col, 0.0), axis=0, keepdims=True)
    low = shard * TOK
    pos_col = (low + iota2((TOK, 1), 0)).astype(F32)
    start_col = jnp.max(jnp.where(begin_row <= pos_col, begin_row, -1.0), axis=1, keepdims=True)
    pos_row = (low + iota2((1, TOK), 1)).astype(F32)
    start_row = jnp.max(jnp.where(begin_col <= pos_row, begin_col, -1.0), axis=0, keepdims=True)
    same = start_col == start_row
    pair_mask[0] = jnp.where(same & (row >= col), 1.0, 0.0)
    pair_mask[1] = jnp.where(same & (row > col), 1.0, 0.0)
    link_mask[0] = jnp.broadcast_to(jnp.where(start_col < low.astype(F32), 1.0, 0.0), square)
    link_mask[1] = jnp.broadcast_to(jnp.where(start_col == start_col[TOK - 1 :, :], 1.0, 0.0), square)
    for level in range(LEVELS):
        below = ((row >> (level + 1)) == (col >> (level + 1))) & ((row >> level) > (col >> level))
        level_mask[level] = jnp.where(below, 1.0, 0.0).astype(BF16)
    level_mask[LEVELS] = jnp.where(row == col, 1.0, 0.0).astype(BF16)
    return begin_col, start_col, pos_col


def prepare_bias(found, shard, bias):
    begin_col, start_col, pos_col = found
    keys = (SPAN + 1) * TOK
    pos_row = ((shard - SPAN) * TOK + iota2((1, keys), 1)).astype(F32)
    start_row = jnp.max(jnp.where(begin_col <= pos_row, begin_col, -1.0), axis=0, keepdims=True)
    visible = (start_col == start_row) & (pos_row <= pos_col)
    bias[...] = jnp.where(visible, 0.0, FAR)


def delta_pairs(heads, refs, pair_mask, link_mask):
    key_ref, value_ref, decay_ref, beta_ref = refs
    square = (TOK, TOK)
    row, col = iota2(square, 0), iota2(square, 1)
    lower = jnp.where(row >= col, 1.0, 0.0).astype(BF16)
    strict = pair_mask[1] > 0.5
    link, tail = link_mask[0], link_mask[1]
    link_last = link[TOK - 1 :, :]
    beta_cols = beta_ref[...].T
    parts = []
    for h in range(heads):
        lanes = slice(h * WIDTH, (h + 1) * WIDTH)
        decay = decay_ref[:, lanes]
        high = decay.astype(BF16)
        rest = decay - high.astype(F32)
        mid = rest.astype(BF16)
        low = (rest - mid.astype(F32)).astype(BF16)
        cum = mul(lower, high) + mul(lower, mid) + mul(lower, low)
        centre, end = cum[TOK // 2 - 1 : TOK // 2, :], cum[TOK - 1 :, :]
        grow, shrink = jnp.exp(cum - centre), jnp.exp(centre - cum)
        from_start, to_end = jnp.exp(centre), jnp.exp(end - centre)
        key = key_ref[:, lanes]
        key = key * lax.rsqrt(jnp.sum(key * key, axis=1, keepdims=True) + EPS)
        key_grow, key_shrink = key * grow, key * shrink
        shrunk = halves(key_shrink)
        pairs = three(mul_nt, halves(key_grow), shrunk)
        beta = beta_cols[:, h : h + 1]
        in_scale = link * from_start
        parts.append(
            dict(
                grow=grow,
                shrunk=shrunk,
                in_scale=in_scale,
                system=halves(jnp.where(strict, pairs, 0.0) * beta),
                right=jnp.concatenate(
                    [value_ref[:, lanes] * beta, key_grow * in_scale * beta], axis=1
                ),
                tail=halves(key_shrink * (tail * to_end)),
                end=jnp.exp(end) * link_last,
            )
        )
    return parts


def delta_solve(parts, level_mask, a_ref, c_ref, midway, finished):
    square = (TOK, TOK)
    row, col = iota2(square, 0), iota2(square, 1)
    system = [part["system"] for part in parts]
    right = [part["right"] for part in parts]
    span = range(len(parts))
    inverse = [level_mask[LEVELS] - system[h][0] * level_mask[0] for h in span]
    for level in range(1, LEVELS):
        if level == 1:
            midway()
        inner = [mul(system[h][0] * level_mask[level], inverse[h]).astype(BF16) for h in span]
        inverse = [inverse[h] - mul(inverse[h], inner[h]).astype(BF16) for h in span]
    solved = [mul(inverse[h], right[h].astype(BF16)) for h in span]
    rest = [right[h] - solved[h] - three(mul, system[h], halves(solved[h])) for h in span]
    solved = [halves(solved[h] + mul(inverse[h], rest[h].astype(BF16))) for h in span]
    for group in range(len(parts) // BATCH):
        for h in range(group * BATCH, (group + 1) * BATCH):
            change = three(mul_tn, parts[h]["tail"], solved[h])
            c_ref[h] = change[:, :WIDTH]
            a_ref[h] = (jnp.where(row == col, parts[h]["end"], 0.0) - change[:, WIDTH:]).astype(BF16)
        finished(group)
    return solved


def delta_outputs(parts, solved, query_ref, pair_mask, left_ref, base_ref):
    incl = pair_mask[0] > 0.5
    for h, part in enumerate(parts):
        lanes = slice(h * WIDTH, (h + 1) * WIDTH)
        query = query_ref[:, lanes]
        query = query * lax.rsqrt(jnp.sum(query * query, axis=1, keepdims=True) + EPS)
        query = query * part["grow"]
        weight = jnp.where(incl, three(mul_nt, halves(query), part["shrunk"]), 0.0)
        output = three(mul, halves(weight), solved[h])
        base_ref[:, lanes] = output[:, :WIDTH]
        left_ref[h] = (query * part["in_scale"] - output[:, WIDTH:]).astype(BF16)


def latent_part(first, heads, scale, query_rows, keys, bias, up_ref, out_ref):
    rows = heads * TOK
    scores = mul_nt(query_rows[first * TOK : first * TOK + rows, :], keys[...])
    mask = jnp.concatenate([bias[...]] * heads, axis=0)
    scores = scores * scale + mask
    top = jnp.max(scores, axis=1, keepdims=True)
    weights = jnp.exp(scores - top)
    totals = jnp.sum(weights, axis=1, keepdims=True)
    context = mul(weights.astype(BF16), keys[...]) * (1.0 / totals)
    context = context.astype(BF16)
    for h in range(heads):
        at = (first + h) * WIDTH
        out_ref[:, at : at + WIDTH] = mul(
            context[h * TOK : (h + 1) * TOK], up_ref[:, at : at + WIDTH]
        ).astype(BF16)


def body(
    shards, head_devices, heads, scale,
    query_hbm, key_hbm, value_hbm, decay_hbm, beta_hbm, latent_hbm, latq_hbm, up_hbm, lens_hbm,
    base, mla_v,
    query_v, key_v, value_v, decay_v, beta_v, latq_v, up_v, keys, lens_v,
    pair_mask, link_mask, level_mask, bias,
    a_ref, c_ref, left_ref, step_ref, send_buf, recv_buf,
    load_sem, chain_send, chain_recv, near_send, near_recv, side_send, side_recv, twin_send, twin_recv,
):
    shard = lax.axis_index("context")
    side = lax.axis_index("head")
    core = lax.rem(shard, 2)
    chip = shard // 2
    last = shards // 2 - 1
    is_a, is_b = core == 0, core == 1
    rank = latq_v.shape[1]
    quarter = TOK // head_devices
    near = (2, 4)
    batch = BATCH

    def ahead(steps):
        return lax.rem(shard + shards + steps, shards)

    def block_rows(block, place):
        return pl.ds(pl.multiple_of(block * TOK + place * quarter, quarter), quarter)

    pairs = [(lens_hbm, lens_v), (decay_hbm, decay_v), (key_hbm, key_v), (beta_hbm, beta_v)]
    pairs += [(value_hbm, value_v), (query_hbm, query_v), (up_hbm, up_v)]
    pairs += [
        (latq_hbm.at[:, pl.ds(h * rank, rank)], latq_v.at[pl.ds(h * TOK, TOK), :]) for h in range(heads)
    ]
    pairs += [(latent_hbm, keys.at[block_rows(SPAN, side)])]
    loads = [pltpu.make_async_copy(pairs[i][0], pairs[i][1], load_sem.at[i]) for i in range(len(pairs))]
    loads[0].start()
    loads[-1].start()
    for load in loads[1:-1]:
        load.start()

    barrier = pltpu.get_barrier_semaphore()

    def greet(peer):
        pl.semaphore_signal(barrier, inc=1, device_id=peer, device_id_type=MESH)

    for step in range(1, head_devices):
        greet((shard, lax.rem(side + step, head_devices)))
    greet((shard + 1 - 2 * core, side))
    for steps in near:
        @pl.when(shard >= steps)
        def _(steps=steps):
            greet((ahead(-steps), side))

    def one_if(condition):
        return jnp.where(condition, 1, 0).astype(jnp.int32)

    expected = head_devices
    for steps in near:
        expected = expected + one_if(shard + steps < shards)

    def near_copy(i):
        return pltpu.make_async_remote_copy(
            src_ref=latent_hbm, dst_ref=keys.at[block_rows(SPAN - near[i], side)],
            send_sem=near_send.at[i], recv_sem=near_recv.at[i],
            device_id=(ahead(near[i]), side), device_id_type=MESH,
        )

    def side_copy(i, step, place):
        rows = block_rows(SPAN - 2 * i, place)
        at = i * (head_devices - 1) + step - 1
        return pltpu.make_async_remote_copy(
            src_ref=keys.at[rows], dst_ref=keys.at[rows],
            send_sem=side_send.at[at], recv_sem=side_recv.at[at],
            device_id=(shard, lax.rem(side + step, head_devices)), device_id_type=MESH,
        )

    def side_start(i):
        for step in range(1, head_devices):
            side_copy(i, step, side).start()

    def side_arrived(i):
        for step in range(1, head_devices):
            side_copy(i, step, lax.rem(side + head_devices - step, head_devices)).wait_recv()

    def twin_copy(i):
        source = pl.ds(pl.multiple_of((2 * i + 2 * (1 - core)) * TOK, TOK), TOK)
        return pltpu.make_async_remote_copy(
            src_ref=keys.at[source], dst_ref=keys.at[pl.ds((2 * i + 1) * TOK, TOK)],
            send_sem=twin_send.at[i], recv_sem=twin_recv.at[i],
            device_id=(shard + 1 - 2 * core, side), device_id_type=MESH,
        )

    MAP_C, MAP_A, MAP_D, MAP_G, MAP_X, MAP_Y = range(6)
    jump = {MAP_C: 1, MAP_A: 1, MAP_D: 2, MAP_G: 2, MAP_X: -1, MAP_Y: -1}

    def state_copy(kind, group):
        part = pl.ds(group * batch, batch)
        if kind == MAP_A:
            source = a_ref.at[part]
        elif kind in (MAP_X, MAP_Y):
            source = recv_buf.at[MAP_D if kind == MAP_X else MAP_G, part]
        else:
            source = send_buf.at[kind, part]
        return pltpu.make_async_remote_copy(
            src_ref=source, dst_ref=recv_buf.at[kind, part],
            send_sem=chain_send.at[kind, group], recv_sem=chain_recv.at[kind, group],
            device_id=(ahead(jump[kind]), side), device_id_type=MESH,
        )

    def members(group):
        return range(group * batch, (group + 1) * batch)

    def send_state(kind, group, values=None):
        if values is not None:
            for h, value in zip(members(group), values):
                send_buf[kind, h] = value.astype(BF16)
        state_copy(kind, group).start()

    def take_state(kind, group):
        state_copy(kind, group).wait_recv()
        return [recv_buf[kind, h] for h in members(group)]

    sends = {
        MAP_C: is_a,
        MAP_A: is_a,
        MAP_D: is_b & (chip < last),
        MAP_G: is_b & (chip > 0) & (chip < last),
        MAP_X: is_b & (chip > 0),
        MAP_Y: is_b & (chip > 1),
    }
    groups = range(heads // batch)

    def emit(group, incoming):
        for h, state in zip(members(group), incoming):
            lanes = slice(h * WIDTH, (h + 1) * WIDTH)
            base[:, lanes] += mul(left_ref[h], state)

    loads[0].wait()
    found = prepare_masks(lens_v[...], shard, pair_mask, link_mask, level_mask)
    for load in loads[1:5]:
        load.wait()
    parts = delta_pairs(heads, (key_v, value_v, decay_v, beta_v), pair_mask, link_mask)

    def open_links():
        pl.semaphore_wait(barrier, expected)
        for i in range(2):
            @pl.when(shard + near[i] < shards)
            def _(i=i):
                near_copy(i).start()
        loads[-1].wait()
        side_start(0)

    def send_maps(group):
        @pl.when(is_a)
        def _():
            send_state(MAP_C, group, [c_ref[h] for h in members(group)])

    solved = delta_solve(parts, level_mask, a_ref, c_ref, open_links, send_maps)

    @pl.when(is_a)
    def _():
        for group in groups:
            send_state(MAP_A, group)

    loads[5].wait()
    delta_outputs(parts, solved, query_v, pair_mask, left_ref, base)

    @pl.when(is_b & (chip < last))
    def _():
        for group in groups:
            incoming = take_state(MAP_C, group)
            send_state(
                MAP_D, group, [c_ref[h] + mul(a_ref[h], x) for h, x in zip(members(group), incoming)]
            )

    @pl.when(is_b & (chip == last))
    def _():
        for group in groups:
            take_state(MAP_C, group)

    @pl.when(is_b)
    def _():
        for group in groups:
            incoming = take_state(MAP_A, group)
            for h, x in zip(members(group), incoming):
                step_ref[h] = mul(a_ref[h], x).astype(BF16)

    for i in range(2):
        @pl.when(shard >= near[i])
        def _(i=i):
            near_copy(i).wait_recv()

        @pl.when(shard < near[i])
        def _(i=i):
            keys[block_rows(SPAN - near[i], side), :] = jnp.zeros((quarter, rank), BF16)

        side_start(i + 1)

    @pl.when(is_b & (chip > 0) & (chip < last))
    def _():
        for group in groups:
            incoming = take_state(MAP_D, group)
            send_state(MAP_G, group, [mul(step_ref[h], x) for h, x in zip(members(group), incoming)])
            send_state(MAP_X, group)

    @pl.when(is_b & (chip == last))
    def _():
        for group in groups:
            take_state(MAP_D, group)
            send_state(MAP_X, group)

    prepare_bias(found, shard, bias)

    side_arrived(0)

    @pl.when(is_a)
    def _():
        twin_copy(1).start()

    side_arrived(1)

    @pl.when(is_a)
    def _():
        twin_copy(0).start()

    @pl.when(is_b)
    def _():
        twin_copy(1).start()

    side_arrived(2)

    @pl.when(is_b)
    def _():
        twin_copy(0).start()

    for load in loads[6:-1]:
        load.wait()
    for i in range(2):
        twin_copy(i).wait_recv()

    def latent_at(part):
        latent_part(part * 4, 4, scale, latq_v, keys, bias, up_v, mla_v)

    latent_at(0)

    @pl.when(is_b & (chip > 1))
    def _():
        for group in groups:
            take_state(MAP_G, group)
            send_state(MAP_Y, group)

    latent_at(1)

    def start_of(h):
        return recv_buf[MAP_C, h].astype(F32)

    def add_out(group, incoming):
        for h, state in zip(members(group), incoming):
            lanes = slice(h * WIDTH, (h + 1) * WIDTH)
            base[:, lanes] += mul(left_ref[h], state.astype(BF16))

    @pl.when(is_b & (chip == 0))
    def _():
        for group in groups:
            add_out(group, [recv_buf[MAP_C, h] for h in members(group)])

    @pl.when(is_b & (chip == 1))
    def _():
        for group in groups:
            add_out(
                group,
                [start_of(h) + mul(recv_buf[MAP_A, h], recv_buf[MAP_D, h]) for h in members(group)],
            )

    @pl.when(is_b & (chip > 1))
    def _():
        for group in groups:
            add_out(
                group,
                [
                    start_of(h)
                    + mul(recv_buf[MAP_A, h], recv_buf[MAP_D, h])
                    + mul(recv_buf[MAP_A, h], recv_buf[MAP_G, h])
                    for h in members(group)
                ],
            )

    @pl.when(is_a & (chip > 0))
    def _():
        for group in groups:
            emit(group, take_state(MAP_X, group))

    @pl.when(is_a & (chip > 1))
    def _():
        for group in groups:
            emit(group, take_state(MAP_Y, group))

    for i in range(2):
        @pl.when(shard + near[i] < shards)
        def _(i=i):
            near_copy(i).wait_send()

        twin_copy(i).wait_send()
    for i in range(SPAN // 2 + 1):
        for step in range(1, head_devices):
            side_copy(i, step, side).wait_send()
    for kind, condition in sends.items():
        @pl.when(condition)
        def _(kind=kind):
            for group in groups:
                state_copy(kind, group).wait_send()


def write_out(delta_ref, mla_ref, delta_hbm, mla_hbm, sem):
    copies = []
    for source, target in ((delta_ref, delta_hbm), (mla_ref, mla_hbm)):
        step = source.shape[0] // PIECES
        for i in range(PIECES):
            part = pl.ds(i * step, step)
            copies.append(
                pltpu.make_async_copy(source.at[part], target.at[part], sem.at[len(copies)])
            )
    for copy in copies:
        copy.start()
    for copy in copies:
        copy.wait()


def solution(mesh):
    shards = mesh.shape["context"]
    head_devices = mesh.shape["head"]

    def step(query_vec, key_vec, value_vec, log_decay, beta, latent, latent_query, w_uv, doc_lengths):
        rows = query_vec.shape[0]
        heads = beta.shape[1]
        rank = w_uv.shape[0]
        width = query_vec.shape[1]
        keys = (SPAN + 1) * rows
        square = (rows, rows)
        outside = pl.BlockSpec(memory_space=pltpu.HBM)
        inside = pl.BlockSpec(memory_space=pltpu.VMEM)
        dma = pltpu.SemaphoreType.DMA
        side_copies = (SPAN // 2 + 1) * (head_devices - 1)
        inputs = (query_vec, key_vec, value_vec, log_decay, beta.T, latent, latent_query, w_uv, doc_lengths.reshape(1, -1))
        inputs = [pltpu.with_memory_space_constraint(x, pltpu.HBM) for x in inputs]
        delta, mla = pl.pallas_call(
            functools.partial(body, shards, head_devices, heads, WIDTH**-0.5),
            out_shape=(
                jax.ShapeDtypeStruct((rows, width), F32),
                jax.ShapeDtypeStruct((rows, width), BF16),
            ),
            in_specs=[outside] * 9,
            out_specs=(inside, inside),
            scratch_shapes=[
                pltpu.VMEM((rows, width), F32),
                pltpu.VMEM((rows, width), F32),
                pltpu.VMEM((rows, width), F32),
                pltpu.VMEM((rows, width), F32),
                pltpu.VMEM((heads, rows), F32),
                pltpu.VMEM((rows * heads, rank), BF16),
                pltpu.VMEM((rank, width), BF16),
                pltpu.VMEM((keys, rank), BF16),
                pltpu.VMEM((1, doc_lengths.shape[0]), jnp.int32),
                pltpu.VMEM((2,) + square, F32),
                pltpu.VMEM((2,) + square, F32),
                pltpu.VMEM((LEVELS + 1,) + square, BF16),
                pltpu.VMEM((rows, keys), F32),
                pltpu.VMEM((heads,) + square, BF16),
                pltpu.VMEM((heads,) + square, F32),
                pltpu.VMEM((heads,) + square, BF16),
                pltpu.VMEM((heads,) + square, BF16),
                pltpu.VMEM((6, heads) + square, BF16),
                pltpu.VMEM((6, heads) + square, BF16),
                dma((8 + heads,)),
                dma((6, heads // BATCH)),
                dma((6, heads // BATCH)),
                dma((2,)),
                dma((2,)),
                dma((side_copies,)),
                dma((side_copies,)),
                dma((2,)),
                dma((2,)),
            ],
            compiler_params=pltpu.CompilerParams(
                collective_id=0, has_side_effects=True, vmem_limit_bytes=48 * 1024 * 1024
            ),
            cost_estimate=pl.CostEstimate(flops=3_000_000_000, bytes_accessed=6_000_000, transcendentals=1_000_000),
            name="packed_attention",
        )(*inputs)
        anywhere = pl.BlockSpec(memory_space=pl.ANY)
        return pl.pallas_call(
            write_out,
            out_shape=(
                jax.ShapeDtypeStruct((rows, width), F32),
                jax.ShapeDtypeStruct((rows, width), BF16),
            ),
            in_specs=[anywhere, anywhere],
            out_specs=(pl.BlockSpec(memory_space=pltpu.HBM), pl.BlockSpec(memory_space=pltpu.HBM)),
            scratch_shapes=[dma((2 * PIECES,))],
            compiler_params=pltpu.CompilerParams(vmem_limit_bytes=1024 * 1024),
            name="write_out",
        )(delta, mla)

    return jax.shard_map(
        step,
        mesh=mesh,
        in_specs=(
            P("context", "head"),
            P("context", "head"),
            P("context", "head"),
            P("context", "head"),
            P("context", "head"),
            P(("context", "head"), None),
            P("context", "head"),
            P(None, "head"),
            P(),
        ),
        out_specs=(P("context", "head"), P("context", "head")),
        check_vma=False,
    )
```

```python
import functools

import jax
import jax.numpy as jnp
from jax import lax
from jax.experimental import pallas as pl
from jax.experimental.pallas import tpu as pltpu
from jax.sharding import PartitionSpec as P

MESH = pl.DeviceIdType.MESH
F32 = jnp.float32
BF16 = jnp.bfloat16
FAR = -1e30
EPS = 1e-6
SPAN = 4
TOK = 128
WIDTH = 128
LEVELS = 7
BATCH = 4
PIECES = 2


def mul(left, right):
    return lax.dot_general(left, right, (((1,), (0,)), ((), ())), preferred_element_type=F32)


def mul_nt(left, right):
    return lax.dot_general(left, right, (((1,), (1,)), ((), ())), preferred_element_type=F32)


def mul_tn(left, right):
    return lax.dot_general(left, right, (((0,), (0,)), ((), ())), preferred_element_type=F32)


def halves(matrix):
    high = matrix.astype(BF16)
    return high, (matrix - high.astype(F32)).astype(BF16)


def three(product, left, right):
    return product(left[0], right[0]) + product(left[1], right[0]) + product(left[0], right[1])


def iota2(shape, axis):
    return lax.broadcasted_iota(jnp.int32, shape, axis)


def prepare_masks(lens, shard, pair_mask, link_mask, level_mask):
    square = (TOK, TOK)
    row, col = iota2(square, 0), iota2(square, 1)
    lens_f = lens.astype(F32)
    lens_row = jnp.broadcast_to(lens_f, square)
    begin_col = jnp.sum(jnp.where(col < row, lens_row, 0.0), axis=1, keepdims=True)
    lens_col = jnp.sum(jnp.where(col == row, lens_row, 0.0), axis=1, keepdims=True)
    begin_row = jnp.sum(jnp.where(row < col, lens_col, 0.0), axis=0, keepdims=True)
    low = shard * TOK
    pos_col = (low + iota2((TOK, 1), 0)).astype(F32)
    start_col = jnp.max(jnp.where(begin_row <= pos_col, begin_row, -1.0), axis=1, keepdims=True)
    pos_row = (low + iota2((1, TOK), 1)).astype(F32)
    start_row = jnp.max(jnp.where(begin_col <= pos_row, begin_col, -1.0), axis=0, keepdims=True)
    same = start_col == start_row
    pair_mask[0] = jnp.where(same & (row >= col), 1.0, 0.0)
    pair_mask[1] = jnp.where(same & (row > col), 1.0, 0.0)
    link_mask[0] = jnp.broadcast_to(jnp.where(start_col < low.astype(F32), 1.0, 0.0), square)
    link_mask[1] = jnp.broadcast_to(jnp.where(start_col == start_col[TOK - 1 :, :], 1.0, 0.0), square)
    for level in range(LEVELS):
        below = ((row >> (level + 1)) == (col >> (level + 1))) & ((row >> level) > (col >> level))
        level_mask[level] = jnp.where(below, 1.0, 0.0).astype(BF16)
    level_mask[LEVELS] = jnp.where(row == col, 1.0, 0.0).astype(BF16)
    return begin_col, start_col, pos_col


def prepare_bias(found, shard, bias):
    begin_col, start_col, pos_col = found
    keys = (SPAN + 1) * TOK
    pos_row = ((shard - SPAN) * TOK + iota2((1, keys), 1)).astype(F32)
    start_row = jnp.max(jnp.where(begin_col <= pos_row, begin_col, -1.0), axis=0, keepdims=True)
    visible = (start_col == start_row) & (pos_row <= pos_col)
    bias[...] = jnp.where(visible, 0.0, FAR)


def delta_pairs(heads, refs, pair_mask, link_mask):
    key_ref, value_ref, decay_ref, beta_ref = refs
    square = (TOK, TOK)
    row, col = iota2(square, 0), iota2(square, 1)
    lower = jnp.where(row >= col, 1.0, 0.0).astype(BF16)
    strict = pair_mask[1] > 0.5
    link, tail = link_mask[0], link_mask[1]
    link_last = link[TOK - 1 :, :]
    beta_cols = beta_ref[...].T
    parts = []
    for h in range(heads):
        lanes = slice(h * WIDTH, (h + 1) * WIDTH)
        decay = decay_ref[:, lanes]
        high = decay.astype(BF16)
        rest = decay - high.astype(F32)
        mid = rest.astype(BF16)
        low = (rest - mid.astype(F32)).astype(BF16)
        cum = mul(lower, high) + mul(lower, mid) + mul(lower, low)
        centre, end = cum[TOK // 2 - 1 : TOK // 2, :], cum[TOK - 1 :, :]
        grow, shrink = jnp.exp(cum - centre), jnp.exp(centre - cum)
        from_start, to_end = jnp.exp(centre), jnp.exp(end - centre)
        key = key_ref[:, lanes]
        key = key * lax.rsqrt(jnp.sum(key * key, axis=1, keepdims=True) + EPS)
        key_grow, key_shrink = key * grow, key * shrink
        shrunk = halves(key_shrink)
        pairs = three(mul_nt, halves(key_grow), shrunk)
        beta = beta_cols[:, h : h + 1]
        in_scale = link * from_start
        parts.append(
            dict(
                grow=grow,
                shrunk=shrunk,
                in_scale=in_scale,
                system=halves(jnp.where(strict, pairs, 0.0) * beta),
                right=jnp.concatenate(
                    [value_ref[:, lanes] * beta, key_grow * in_scale * beta], axis=1
                ),
                tail=halves(key_shrink * (tail * to_end)),
                end=jnp.exp(end) * link_last,
            )
        )
    return parts


def delta_solve(parts, level_mask, a_ref, c_ref, midway, finished):
    square = (TOK, TOK)
    row, col = iota2(square, 0), iota2(square, 1)
    system = [part["system"] for part in parts]
    right = [part["right"] for part in parts]
    span = range(len(parts))
    inverse = [level_mask[LEVELS] - system[h][0] * level_mask[0] for h in span]
    for level in range(1, LEVELS):
        if level == 1:
            midway()
        inner = [mul(system[h][0] * level_mask[level], inverse[h]).astype(BF16) for h in span]
        inverse = [inverse[h] - mul(inverse[h], inner[h]).astype(BF16) for h in span]
    solved = [mul(inverse[h], right[h].astype(BF16)) for h in span]
    rest = [right[h] - solved[h] - three(mul, system[h], halves(solved[h])) for h in span]
    solved = [halves(solved[h] + mul(inverse[h], rest[h].astype(BF16))) for h in span]
    for group in range(len(parts) // BATCH):
        for h in range(group * BATCH, (group + 1) * BATCH):
            change = three(mul_tn, parts[h]["tail"], solved[h])
            c_ref[h] = change[:, :WIDTH]
            a_ref[h] = (jnp.where(row == col, parts[h]["end"], 0.0) - change[:, WIDTH:]).astype(BF16)
        finished(group)
    return solved


def delta_outputs(parts, solved, query_ref, pair_mask, left_ref, base_ref):
    incl = pair_mask[0] > 0.5
    for h, part in enumerate(parts):
        lanes = slice(h * WIDTH, (h + 1) * WIDTH)
        query = query_ref[:, lanes]
        query = query * lax.rsqrt(jnp.sum(query * query, axis=1, keepdims=True) + EPS)
        query = query * part["grow"]
        weight = jnp.where(incl, three(mul_nt, halves(query), part["shrunk"]), 0.0)
        output = three(mul, halves(weight), solved[h])
        base_ref[:, lanes] = output[:, :WIDTH]
        left_ref[h] = (query * part["in_scale"] - output[:, WIDTH:]).astype(BF16)


def latent_scores(first, heads, scale, query_rows, keys, bias):
    rows = query_rows[first * TOK : (first + heads) * TOK, :]
    return mul_nt(rows, keys[...]) * scale + jnp.concatenate([bias[...]] * heads, axis=0)


def latent_finish(first, heads, scores, keys, up_ref, out_ref):
    top = jnp.max(scores, axis=1, keepdims=True)
    weights = jnp.exp(scores - top)
    totals = jnp.sum(weights, axis=1, keepdims=True)
    context = mul(weights.astype(BF16), keys[...]) * (1.0 / totals)
    context = context.astype(BF16)
    for h in range(heads):
        at = (first + h) * WIDTH
        out_ref[:, at : at + WIDTH] = mul(
            context[h * TOK : (h + 1) * TOK], up_ref[:, at : at + WIDTH]
        ).astype(BF16)


def body(
    shards, head_devices, heads, scale,
    query_hbm, key_hbm, value_hbm, decay_hbm, beta_hbm, latent_hbm, latq_hbm, up_hbm, lens_hbm,
    base, mla_v,
    query_v, key_v, value_v, decay_v, beta_v, latq_v, up_v, keys, lens_v,
    pair_mask, link_mask, level_mask, bias,
    a_ref, c_ref, left_ref, step_ref, send_buf, recv_buf,
    load_sem, chain_send, chain_recv, near_send, near_recv, side_send, side_recv, twin_send, twin_recv,
):
    shard = lax.axis_index("context")
    side = lax.axis_index("head")
    core = lax.rem(shard, 2)
    chip = shard // 2
    last = shards // 2 - 1
    is_a, is_b = core == 0, core == 1
    rank = latq_v.shape[1]
    quarter = TOK // head_devices
    near = (2, 4)
    batch = BATCH

    def ahead(steps):
        return lax.rem(shard + shards + steps, shards)

    def block_rows(block, place):
        return pl.ds(pl.multiple_of(block * TOK + place * quarter, quarter), quarter)

    pairs = [(lens_hbm, lens_v), (decay_hbm, decay_v), (key_hbm, key_v), (beta_hbm, beta_v)]
    pairs += [(value_hbm, value_v), (query_hbm, query_v), (up_hbm, up_v)]
    pairs += [
        (latq_hbm.at[:, pl.ds(h * rank, rank)], latq_v.at[pl.ds(h * TOK, TOK), :]) for h in range(heads)
    ]
    pairs += [(latent_hbm, keys.at[block_rows(SPAN, side)])]
    loads = [pltpu.make_async_copy(pairs[i][0], pairs[i][1], load_sem.at[i]) for i in range(len(pairs))]
    loads[0].start()
    loads[-1].start()
    for load in loads[1:-1]:
        load.start()

    barrier = pltpu.get_barrier_semaphore()

    def greet(peer):
        pl.semaphore_signal(barrier, inc=1, device_id=peer, device_id_type=MESH)

    for step in range(1, head_devices):
        greet((shard, lax.rem(side + step, head_devices)))
    greet((shard + 1 - 2 * core, side))
    for steps in near:
        @pl.when(shard >= steps)
        def _(steps=steps):
            greet((ahead(-steps), side))

    def one_if(condition):
        return jnp.where(condition, 1, 0).astype(jnp.int32)

    expected = head_devices
    for steps in near:
        expected = expected + one_if(shard + steps < shards)

    def near_copy(i):
        return pltpu.make_async_remote_copy(
            src_ref=latent_hbm, dst_ref=keys.at[block_rows(SPAN - near[i], side)],
            send_sem=near_send.at[i], recv_sem=near_recv.at[i],
            device_id=(ahead(near[i]), side), device_id_type=MESH,
        )

    def side_copy(i, step, place):
        rows = block_rows(SPAN - 2 * i, place)
        at = i * (head_devices - 1) + step - 1
        return pltpu.make_async_remote_copy(
            src_ref=keys.at[rows], dst_ref=keys.at[rows],
            send_sem=side_send.at[at], recv_sem=side_recv.at[at],
            device_id=(shard, lax.rem(side + step, head_devices)), device_id_type=MESH,
        )

    def side_start(i):
        for step in range(1, head_devices):
            side_copy(i, step, side).start()

    def side_arrived(i):
        for step in range(1, head_devices):
            side_copy(i, step, lax.rem(side + head_devices - step, head_devices)).wait_recv()

    def twin_copy(i):
        source = pl.ds(pl.multiple_of((2 * i + 2 * (1 - core)) * TOK, TOK), TOK)
        return pltpu.make_async_remote_copy(
            src_ref=keys.at[source], dst_ref=keys.at[pl.ds((2 * i + 1) * TOK, TOK)],
            send_sem=twin_send.at[i], recv_sem=twin_recv.at[i],
            device_id=(shard + 1 - 2 * core, side), device_id_type=MESH,
        )

    MAP_C, MAP_A, MAP_D, MAP_G, MAP_X, MAP_Y = range(6)
    jump = {MAP_C: 1, MAP_A: 1, MAP_D: 2, MAP_G: 2, MAP_X: -1, MAP_Y: -1}

    def state_copy(kind, group):
        part = pl.ds(group * batch, batch)
        if kind == MAP_A:
            source = a_ref.at[part]
        elif kind in (MAP_X, MAP_Y):
            source = recv_buf.at[MAP_D if kind == MAP_X else MAP_G, part]
        else:
            source = send_buf.at[kind, part]
        return pltpu.make_async_remote_copy(
            src_ref=source, dst_ref=recv_buf.at[kind, part],
            send_sem=chain_send.at[kind, group], recv_sem=chain_recv.at[kind, group],
            device_id=(ahead(jump[kind]), side), device_id_type=MESH,
        )

    def members(group):
        return range(group * batch, (group + 1) * batch)

    def send_state(kind, group, values=None):
        if values is not None:
            for h, value in zip(members(group), values):
                send_buf[kind, h] = value.astype(BF16)
        state_copy(kind, group).start()

    def take_state(kind, group):
        state_copy(kind, group).wait_recv()
        return [recv_buf[kind, h] for h in members(group)]

    sends = {
        MAP_C: is_a,
        MAP_A: is_a,
        MAP_D: is_b & (chip < last),
        MAP_G: is_b & (chip > 0) & (chip < last),
        MAP_X: is_b & (chip > 0),
        MAP_Y: is_b & (chip > 1),
    }
    groups = range(heads // batch)

    def emit(group, incoming):
        for h, state in zip(members(group), incoming):
            lanes = slice(h * WIDTH, (h + 1) * WIDTH)
            base[:, lanes] += mul(left_ref[h], state)

    loads[0].wait()
    found = prepare_masks(lens_v[...], shard, pair_mask, link_mask, level_mask)
    for load in loads[1:5]:
        load.wait()
    parts = delta_pairs(heads, (key_v, value_v, decay_v, beta_v), pair_mask, link_mask)

    def open_links():
        pl.semaphore_wait(barrier, expected)
        for i in range(2):
            @pl.when(shard + near[i] < shards)
            def _(i=i):
                near_copy(i).start()
        loads[-1].wait()
        side_start(0)

    def send_maps(group):
        @pl.when(is_a)
        def _():
            send_state(MAP_C, group, [c_ref[h] for h in members(group)])

    solved = delta_solve(parts, level_mask, a_ref, c_ref, open_links, send_maps)

    @pl.when(is_a)
    def _():
        for group in groups:
            send_state(MAP_A, group)

    loads[5].wait()
    delta_outputs(parts, solved, query_v, pair_mask, left_ref, base)

    @pl.when(is_b & (chip < last))
    def _():
        for group in groups:
            incoming = take_state(MAP_C, group)
            send_state(
                MAP_D, group, [c_ref[h] + mul(a_ref[h], x) for h, x in zip(members(group), incoming)]
            )

    @pl.when(is_b & (chip == last))
    def _():
        for group in groups:
            take_state(MAP_C, group)

    @pl.when(is_b)
    def _():
        for group in groups:
            incoming = take_state(MAP_A, group)
            for h, x in zip(members(group), incoming):
                step_ref[h] = mul(a_ref[h], x).astype(BF16)

    for i in range(2):
        @pl.when(shard >= near[i])
        def _(i=i):
            near_copy(i).wait_recv()

        @pl.when(shard < near[i])
        def _(i=i):
            keys[block_rows(SPAN - near[i], side), :] = jnp.zeros((quarter, rank), BF16)

        side_start(i + 1)

    @pl.when(is_b & (chip > 0) & (chip < last))
    def _():
        for group in groups:
            incoming = take_state(MAP_D, group)
            send_state(MAP_G, group, [mul(step_ref[h], x) for h, x in zip(members(group), incoming)])
            send_state(MAP_X, group)

    @pl.when(is_b & (chip == last))
    def _():
        for group in groups:
            take_state(MAP_D, group)
            send_state(MAP_X, group)

    prepare_bias(found, shard, bias)

    side_arrived(0)

    @pl.when(is_a)
    def _():
        twin_copy(1).start()

    side_arrived(1)

    @pl.when(is_a)
    def _():
        twin_copy(0).start()

    @pl.when(is_b)
    def _():
        twin_copy(1).start()

    side_arrived(2)

    @pl.when(is_b)
    def _():
        twin_copy(0).start()

    for load in loads[6:-1]:
        load.wait()
    for i in range(2):
        twin_copy(i).wait_recv()

    half = heads // 2
    scores = [latent_scores(part * half, half, scale, latq_v, keys, bias) for part in range(2)]
    latent_finish(0, half, scores[0], keys, up_v, mla_v)

    @pl.when(is_b & (chip > 1))
    def _():
        for group in groups:
            take_state(MAP_G, group)
            send_state(MAP_Y, group)

    latent_finish(half, half, scores[1], keys, up_v, mla_v)

    def start_of(h):
        return recv_buf[MAP_C, h].astype(F32)

    def add_out(group, incoming):
        for h, state in zip(members(group), incoming):
            lanes = slice(h * WIDTH, (h + 1) * WIDTH)
            base[:, lanes] += mul(left_ref[h], state.astype(BF16))

    @pl.when(is_b & (chip == 0))
    def _():
        for group in groups:
            add_out(group, [recv_buf[MAP_C, h] for h in members(group)])

    @pl.when(is_b & (chip == 1))
    def _():
        for group in groups:
            add_out(
                group,
                [start_of(h) + mul(recv_buf[MAP_A, h], recv_buf[MAP_D, h]) for h in members(group)],
            )

    @pl.when(is_b & (chip > 1))
    def _():
        for group in groups:
            add_out(
                group,
                [
                    start_of(h)
                    + mul(recv_buf[MAP_A, h], recv_buf[MAP_D, h])
                    + mul(recv_buf[MAP_A, h], recv_buf[MAP_G, h])
                    for h in members(group)
                ],
            )

    @pl.when(is_a & (chip > 0))
    def _():
        for group in groups:
            emit(group, take_state(MAP_X, group))

    @pl.when(is_a & (chip > 1))
    def _():
        for group in groups:
            emit(group, take_state(MAP_Y, group))

    for i in range(2):
        @pl.when(shard + near[i] < shards)
        def _(i=i):
            near_copy(i).wait_send()

        twin_copy(i).wait_send()
    for i in range(SPAN // 2 + 1):
        for step in range(1, head_devices):
            side_copy(i, step, side).wait_send()
    for kind, condition in sends.items():
        @pl.when(condition)
        def _(kind=kind):
            for group in groups:
                state_copy(kind, group).wait_send()


def write_out(delta_ref, mla_ref, delta_hbm, mla_hbm, sem):
    copies = []
    for source, target in ((delta_ref, delta_hbm), (mla_ref, mla_hbm)):
        step = source.shape[0] // PIECES
        for i in range(PIECES):
            part = pl.ds(i * step, step)
            copies.append(
                pltpu.make_async_copy(source.at[part], target.at[part], sem.at[len(copies)])
            )
    for copy in copies:
        copy.start()
    for copy in copies:
        copy.wait()


def solution(mesh):
    shards = mesh.shape["context"]
    head_devices = mesh.shape["head"]

    def step(query_vec, key_vec, value_vec, log_decay, beta, latent, latent_query, w_uv, doc_lengths):
        rows = query_vec.shape[0]
        heads = beta.shape[1]
        rank = w_uv.shape[0]
        width = query_vec.shape[1]
        keys = (SPAN + 1) * rows
        square = (rows, rows)
        outside = pl.BlockSpec(memory_space=pltpu.HBM)
        inside = pl.BlockSpec(memory_space=pltpu.VMEM)
        dma = pltpu.SemaphoreType.DMA
        side_copies = (SPAN // 2 + 1) * (head_devices - 1)
        inputs = (query_vec, key_vec, value_vec, log_decay, beta.T, latent, latent_query, w_uv, doc_lengths.reshape(1, -1))
        inputs = [pltpu.with_memory_space_constraint(x, pltpu.HBM) for x in inputs]
        delta, mla = pl.pallas_call(
            functools.partial(body, shards, head_devices, heads, WIDTH**-0.5),
            out_shape=(
                jax.ShapeDtypeStruct((rows, width), F32),
                jax.ShapeDtypeStruct((rows, width), BF16),
            ),
            in_specs=[outside] * 9,
            out_specs=(inside, inside),
            scratch_shapes=[
                pltpu.VMEM((rows, width), F32),
                pltpu.VMEM((rows, width), F32),
                pltpu.VMEM((rows, width), F32),
                pltpu.VMEM((rows, width), F32),
                pltpu.VMEM((heads, rows), F32),
                pltpu.VMEM((rows * heads, rank), BF16),
                pltpu.VMEM((rank, width), BF16),
                pltpu.VMEM((keys, rank), BF16),
                pltpu.VMEM((1, doc_lengths.shape[0]), jnp.int32),
                pltpu.VMEM((2,) + square, F32),
                pltpu.VMEM((2,) + square, F32),
                pltpu.VMEM((LEVELS + 1,) + square, BF16),
                pltpu.VMEM((rows, keys), F32),
                pltpu.VMEM((heads,) + square, BF16),
                pltpu.VMEM((heads,) + square, F32),
                pltpu.VMEM((heads,) + square, BF16),
                pltpu.VMEM((heads,) + square, BF16),
                pltpu.VMEM((6, heads) + square, BF16),
                pltpu.VMEM((6, heads) + square, BF16),
                dma((8 + heads,)),
                dma((6, heads // BATCH)),
                dma((6, heads // BATCH)),
                dma((2,)),
                dma((2,)),
                dma((side_copies,)),
                dma((side_copies,)),
                dma((2,)),
                dma((2,)),
            ],
            compiler_params=pltpu.CompilerParams(
                collective_id=0, has_side_effects=True, vmem_limit_bytes=48 * 1024 * 1024
            ),
            cost_estimate=pl.CostEstimate(flops=3_000_000_000, bytes_accessed=6_000_000, transcendentals=1_000_000),
            name="packed_attention",
        )(*inputs)
        anywhere = pl.BlockSpec(memory_space=pl.ANY)
        return pl.pallas_call(
            write_out,
            out_shape=(
                jax.ShapeDtypeStruct((rows, width), F32),
                jax.ShapeDtypeStruct((rows, width), BF16),
            ),
            in_specs=[anywhere, anywhere],
            out_specs=(pl.BlockSpec(memory_space=pltpu.HBM), pl.BlockSpec(memory_space=pltpu.HBM)),
            scratch_shapes=[dma((2 * PIECES,))],
            compiler_params=pltpu.CompilerParams(vmem_limit_bytes=1024 * 1024),
            name="write_out",
        )(delta, mla)

    return jax.shard_map(
        step,
        mesh=mesh,
        in_specs=(
            P("context", "head"),
            P("context", "head"),
            P("context", "head"),
            P("context", "head"),
            P("context", "head"),
            P(("context", "head"), None),
            P("context", "head"),
            P(None, "head"),
            P(),
        ),
        out_specs=(P("context", "head"), P("context", "head")),
        check_vma=False,
    )
```

```python
import functools

import jax
import jax.numpy as jnp
from jax import lax
from jax.experimental import pallas as pl
from jax.experimental.pallas import tpu as pltpu
from jax.sharding import PartitionSpec as P

MESH = pl.DeviceIdType.MESH
F32 = jnp.float32
BF16 = jnp.bfloat16
FAR = -1e30
EPS = 1e-6
SPAN = 4
TOK = 128
WIDTH = 128
LEVELS = 7
BATCH = 4
PIECES = 2


def mul(left, right):
    return lax.dot_general(left, right, (((1,), (0,)), ((), ())), preferred_element_type=F32)


def mul_nt(left, right):
    return lax.dot_general(left, right, (((1,), (1,)), ((), ())), preferred_element_type=F32)


def mul_tn(left, right):
    return lax.dot_general(left, right, (((0,), (0,)), ((), ())), preferred_element_type=F32)


def halves(matrix):
    high = matrix.astype(BF16)
    return high, (matrix - high.astype(F32)).astype(BF16)


def three(product, left, right):
    return product(left[0], right[0]) + product(left[1], right[0]) + product(left[0], right[1])


def iota2(shape, axis):
    return lax.broadcasted_iota(jnp.int32, shape, axis)


def prepare_masks(lens, shard, pair_mask, link_mask, level_mask):
    square = (TOK, TOK)
    row, col = iota2(square, 0), iota2(square, 1)
    lens_f = lens.astype(F32)
    lens_row = jnp.broadcast_to(lens_f, square)
    begin_col = jnp.sum(jnp.where(col < row, lens_row, 0.0), axis=1, keepdims=True)
    lens_col = jnp.sum(jnp.where(col == row, lens_row, 0.0), axis=1, keepdims=True)
    begin_row = jnp.sum(jnp.where(row < col, lens_col, 0.0), axis=0, keepdims=True)
    low = shard * TOK
    pos_col = (low + iota2((TOK, 1), 0)).astype(F32)
    start_col = jnp.max(jnp.where(begin_row <= pos_col, begin_row, -1.0), axis=1, keepdims=True)
    pos_row = (low + iota2((1, TOK), 1)).astype(F32)
    start_row = jnp.max(jnp.where(begin_col <= pos_row, begin_col, -1.0), axis=0, keepdims=True)
    same = start_col == start_row
    pair_mask[0] = jnp.where(same & (row >= col), 1.0, 0.0)
    pair_mask[1] = jnp.where(same & (row > col), 1.0, 0.0)
    link_mask[0] = jnp.broadcast_to(jnp.where(start_col < low.astype(F32), 1.0, 0.0), square)
    link_mask[1] = jnp.broadcast_to(jnp.where(start_col == start_col[TOK - 1 :, :], 1.0, 0.0), square)
    for level in range(LEVELS):
        below = ((row >> (level + 1)) == (col >> (level + 1))) & ((row >> level) > (col >> level))
        level_mask[level] = jnp.where(below, 1.0, 0.0).astype(BF16)
    level_mask[LEVELS] = jnp.where(row == col, 1.0, 0.0).astype(BF16)
    return begin_col, start_col, pos_col


def prepare_bias(found, shard, bias):
    begin_col, start_col, pos_col = found
    keys = (SPAN + 1) * TOK
    pos_row = ((shard - SPAN) * TOK + iota2((1, keys), 1)).astype(F32)
    start_row = jnp.max(jnp.where(begin_col <= pos_row, begin_col, -1.0), axis=0, keepdims=True)
    visible = (start_col == start_row) & (pos_row <= pos_col)
    bias[...] = jnp.where(visible, 0.0, FAR)


def delta_pairs(heads, refs, pair_mask, link_mask):
    key_ref, value_ref, decay_ref, beta_ref = refs
    square = (TOK, TOK)
    row, col = iota2(square, 0), iota2(square, 1)
    lower = jnp.where(row >= col, 1.0, 0.0).astype(BF16)
    strict = pair_mask[1] > 0.5
    link, tail = link_mask[0], link_mask[1]
    link_last = link[TOK - 1 :, :]
    beta_cols = beta_ref[...].T
    parts = []
    for h in range(heads):
        lanes = slice(h * WIDTH, (h + 1) * WIDTH)
        decay = decay_ref[:, lanes]
        high = decay.astype(BF16)
        rest = decay - high.astype(F32)
        mid = rest.astype(BF16)
        low = (rest - mid.astype(F32)).astype(BF16)
        cum = mul(lower, high) + mul(lower, mid) + mul(lower, low)
        centre, end = cum[TOK // 2 - 1 : TOK // 2, :], cum[TOK - 1 :, :]
        grow, shrink = jnp.exp(cum - centre), jnp.exp(centre - cum)
        from_start, to_end = jnp.exp(centre), jnp.exp(end - centre)
        key = key_ref[:, lanes]
        key = key * lax.rsqrt(jnp.sum(key * key, axis=1, keepdims=True) + EPS)
        key_grow, key_shrink = key * grow, key * shrink
        shrunk = halves(key_shrink)
        pairs = three(mul_nt, halves(key_grow), shrunk)
        beta = beta_cols[:, h : h + 1]
        in_scale = link * from_start
        parts.append(
            dict(
                grow=grow,
                shrunk=shrunk,
                in_scale=in_scale,
                system=halves(jnp.where(strict, pairs, 0.0) * beta),
                right=jnp.concatenate(
                    [value_ref[:, lanes] * beta, key_grow * in_scale * beta], axis=1
                ),
                tail=halves(key_shrink * (tail * to_end)),
                end=jnp.exp(end) * link_last,
            )
        )
    return parts


def delta_solve(parts, level_mask, a_ref, c_ref, midway, finished):
    square = (TOK, TOK)
    row, col = iota2(square, 0), iota2(square, 1)
    system = [part["system"] for part in parts]
    right = [part["right"] for part in parts]
    span = range(len(parts))
    inverse = [level_mask[LEVELS] - system[h][0] * level_mask[0] for h in span]
    for level in range(1, LEVELS):
        if level == 1:
            midway()
        inner = [mul(system[h][0] * level_mask[level], inverse[h]).astype(BF16) for h in span]
        inverse = [inverse[h] - mul(inverse[h], inner[h]).astype(BF16) for h in span]
    solved = [mul(inverse[h], right[h].astype(BF16)) for h in span]
    rest = [right[h] - solved[h] - three(mul, system[h], halves(solved[h])) for h in span]
    solved = [halves(solved[h] + mul(inverse[h], rest[h].astype(BF16))) for h in span]
    for group in range(len(parts) // BATCH):
        for h in range(group * BATCH, (group + 1) * BATCH):
            change = three(mul_tn, parts[h]["tail"], solved[h])
            c_ref[h] = change[:, :WIDTH]
            a_ref[h] = (jnp.where(row == col, parts[h]["end"], 0.0) - change[:, WIDTH:]).astype(BF16)
        finished(group)
    return solved


def delta_outputs(parts, solved, query_ref, pair_mask, left_ref, base_ref):
    incl = pair_mask[0] > 0.5
    for h, part in enumerate(parts):
        lanes = slice(h * WIDTH, (h + 1) * WIDTH)
        query = query_ref[:, lanes]
        query = query * lax.rsqrt(jnp.sum(query * query, axis=1, keepdims=True) + EPS)
        query = query * part["grow"]
        weight = jnp.where(incl, three(mul_nt, halves(query), part["shrunk"]), 0.0)
        output = three(mul, halves(weight), solved[h])
        base_ref[:, lanes] = output[:, :WIDTH]
        left_ref[h] = (query * part["in_scale"] - output[:, WIDTH:]).astype(BF16)


def latent_scores(first, heads, scale, query_rows, keys, bias):
    rows = query_rows[first * TOK : (first + heads) * TOK, :]
    return mul_nt(rows, keys[...]) * scale + jnp.concatenate([bias[...]] * heads, axis=0)


def latent_finish(first, heads, scores, keys, up_ref, out_ref):
    top = jnp.max(scores, axis=1, keepdims=True)
    weights = jnp.exp(scores - top)
    totals = jnp.sum(weights, axis=1, keepdims=True)
    context = mul(weights.astype(BF16), keys[...]) * (1.0 / totals)
    context = context.astype(BF16)
    for h in range(heads):
        at = (first + h) * WIDTH
        out_ref[:, at : at + WIDTH] = mul(
            context[h * TOK : (h + 1) * TOK], up_ref[:, at : at + WIDTH]
        ).astype(BF16)


def body(
    shards, head_devices, heads, scale,
    query_hbm, key_hbm, value_hbm, decay_hbm, beta_hbm, latent_hbm, latq_hbm, up_hbm, lens_hbm,
    base, mla_v,
    query_v, key_v, value_v, decay_v, beta_v, latq_v, up_v, keys, lens_v,
    pair_mask, link_mask, level_mask, bias,
    a_ref, c_ref, left_ref, step_ref, send_buf, recv_buf,
    load_sem, chain_send, chain_recv, near_send, near_recv, side_send, side_recv, twin_send, twin_recv,
):
    shard = lax.axis_index("context")
    side = lax.axis_index("head")
    core = lax.rem(shard, 2)
    chip = shard // 2
    last = shards // 2 - 1
    is_a, is_b = core == 0, core == 1
    rank = latq_v.shape[1]
    quarter = TOK // head_devices
    near = (2, 4)
    batch = BATCH

    def ahead(steps):
        return lax.rem(shard + shards + steps, shards)

    def block_rows(block, place):
        return pl.ds(pl.multiple_of(block * TOK + place * quarter, quarter), quarter)

    pairs = [(lens_hbm, lens_v), (decay_hbm, decay_v), (key_hbm, key_v), (beta_hbm, beta_v)]
    pairs += [(value_hbm, value_v), (query_hbm, query_v), (up_hbm, up_v)]
    pairs += [
        (latq_hbm.at[:, pl.ds(h * rank, rank)], latq_v.at[pl.ds(h * TOK, TOK), :]) for h in range(heads)
    ]
    pairs += [(latent_hbm, keys.at[block_rows(SPAN, side)])]
    loads = [pltpu.make_async_copy(pairs[i][0], pairs[i][1], load_sem.at[i]) for i in range(len(pairs))]
    loads[0].start()
    loads[-1].start()
    for load in loads[1:-1]:
        load.start()

    barrier = pltpu.get_barrier_semaphore()

    def greet(peer):
        pl.semaphore_signal(barrier, inc=1, device_id=peer, device_id_type=MESH)

    for step in range(1, head_devices):
        greet((shard, lax.rem(side + step, head_devices)))
    greet((shard + 1 - 2 * core, side))
    for steps in near:
        @pl.when(shard >= steps)
        def _(steps=steps):
            greet((ahead(-steps), side))

    def one_if(condition):
        return jnp.where(condition, 1, 0).astype(jnp.int32)

    expected = head_devices
    for steps in near:
        expected = expected + one_if(shard + steps < shards)

    def near_copy(i):
        return pltpu.make_async_remote_copy(
            src_ref=latent_hbm, dst_ref=keys.at[block_rows(SPAN - near[i], side)],
            send_sem=near_send.at[i], recv_sem=near_recv.at[i],
            device_id=(ahead(near[i]), side), device_id_type=MESH,
        )

    def side_copy(i, step, place):
        rows = block_rows(SPAN - 2 * i, place)
        at = i * (head_devices - 1) + step - 1
        return pltpu.make_async_remote_copy(
            src_ref=keys.at[rows], dst_ref=keys.at[rows],
            send_sem=side_send.at[at], recv_sem=side_recv.at[at],
            device_id=(shard, lax.rem(side + step, head_devices)), device_id_type=MESH,
        )

    def side_start(i):
        for step in range(1, head_devices):
            side_copy(i, step, side).start()

    def side_arrived(i):
        for step in range(1, head_devices):
            side_copy(i, step, lax.rem(side + head_devices - step, head_devices)).wait_recv()

    def twin_copy(i):
        source = pl.ds(pl.multiple_of((2 * i + 2 * (1 - core)) * TOK, TOK), TOK)
        return pltpu.make_async_remote_copy(
            src_ref=keys.at[source], dst_ref=keys.at[pl.ds((2 * i + 1) * TOK, TOK)],
            send_sem=twin_send.at[i], recv_sem=twin_recv.at[i],
            device_id=(shard + 1 - 2 * core, side), device_id_type=MESH,
        )

    MAP_C, MAP_A, MAP_D, MAP_G, MAP_X, MAP_Y = range(6)
    jump = {MAP_C: 1, MAP_A: 1, MAP_D: 2, MAP_G: 2, MAP_X: -1, MAP_Y: -1}

    def state_copy(kind, group):
        part = pl.ds(group * batch, batch)
        if kind == MAP_A:
            source = a_ref.at[part]
        elif kind in (MAP_X, MAP_Y):
            source = recv_buf.at[MAP_D if kind == MAP_X else MAP_G, part]
        else:
            source = send_buf.at[kind, part]
        return pltpu.make_async_remote_copy(
            src_ref=source, dst_ref=recv_buf.at[kind, part],
            send_sem=chain_send.at[kind, group], recv_sem=chain_recv.at[kind, group],
            device_id=(ahead(jump[kind]), side), device_id_type=MESH,
        )

    def members(group):
        return range(group * batch, (group + 1) * batch)

    def send_state(kind, group, values=None):
        if values is not None:
            for h, value in zip(members(group), values):
                send_buf[kind, h] = value.astype(BF16)
        state_copy(kind, group).start()

    def take_state(kind, group):
        state_copy(kind, group).wait_recv()
        return [recv_buf[kind, h] for h in members(group)]

    sends = {
        MAP_C: is_a,
        MAP_A: is_a,
        MAP_D: is_b & (chip < last),
        MAP_G: is_b & (chip > 0) & (chip < last),
        MAP_X: is_b & (chip > 0),
        MAP_Y: is_b & (chip > 1),
    }
    groups = range(heads // batch)

    def emit(group, incoming):
        for h, state in zip(members(group), incoming):
            lanes = slice(h * WIDTH, (h + 1) * WIDTH)
            base[:, lanes] += mul(left_ref[h], state)

    loads[0].wait()
    found = prepare_masks(lens_v[...], shard, pair_mask, link_mask, level_mask)
    for load in loads[1:5]:
        load.wait()
    parts = delta_pairs(heads, (key_v, value_v, decay_v, beta_v), pair_mask, link_mask)

    def open_links():
        pl.semaphore_wait(barrier, expected)
        for i in range(2):
            @pl.when(shard + near[i] < shards)
            def _(i=i):
                near_copy(i).start()
        loads[-1].wait()
        side_start(0)

    def send_maps(group):
        @pl.when(is_a)
        def _():
            send_state(MAP_C, group, [c_ref[h] for h in members(group)])

    solved = delta_solve(parts, level_mask, a_ref, c_ref, open_links, send_maps)

    @pl.when(is_a)
    def _():
        for group in groups:
            send_state(MAP_A, group)

    loads[5].wait()
    delta_outputs(parts, solved, query_v, pair_mask, left_ref, base)

    @pl.when(is_b & (chip < last))
    def _():
        for group in groups:
            incoming = take_state(MAP_C, group)
            send_state(
                MAP_D, group, [c_ref[h] + mul(a_ref[h], x) for h, x in zip(members(group), incoming)]
            )

    @pl.when(is_b & (chip == last))
    def _():
        for group in groups:
            take_state(MAP_C, group)

    @pl.when(is_b)
    def _():
        for group in groups:
            incoming = take_state(MAP_A, group)
            emit(group, [recv_buf[MAP_C, h] for h in members(group)])
            for h, x in zip(members(group), incoming):
                step_ref[h] = mul(a_ref[h], x).astype(BF16)
                left_ref[h] = mul(left_ref[h], x).astype(BF16)

    for i in range(2):
        @pl.when(shard >= near[i])
        def _(i=i):
            near_copy(i).wait_recv()

        @pl.when(shard < near[i])
        def _(i=i):
            keys[block_rows(SPAN - near[i], side), :] = jnp.zeros((quarter, rank), BF16)

        side_start(i + 1)

    @pl.when(is_b & (chip > 0) & (chip < last))
    def _():
        for group in groups:
            incoming = take_state(MAP_D, group)
            send_state(MAP_G, group, [mul(step_ref[h], x) for h, x in zip(members(group), incoming)])
            send_state(MAP_X, group)

    @pl.when(is_b & (chip == last))
    def _():
        for group in groups:
            take_state(MAP_D, group)
            send_state(MAP_X, group)

    prepare_bias(found, shard, bias)

    side_arrived(0)

    @pl.when(is_a)
    def _():
        twin_copy(1).start()

    side_arrived(1)

    @pl.when(is_a)
    def _():
        twin_copy(0).start()

    @pl.when(is_b)
    def _():
        twin_copy(1).start()

    side_arrived(2)

    @pl.when(is_b)
    def _():
        twin_copy(0).start()

    @pl.when(is_a & (chip > 0))
    def _():
        for group in groups:
            emit(group, take_state(MAP_X, group))

    @pl.when(is_b & (chip > 0))
    def _():
        for group in groups:
            emit(group, [recv_buf[MAP_D, h] for h in members(group)])

    for load in loads[6:-1]:
        load.wait()
    for i in range(2):
        twin_copy(i).wait_recv()

    half = heads // 2
    scores = [latent_scores(part * half, half, scale, latq_v, keys, bias) for part in range(2)]
    latent_finish(0, half, scores[0], keys, up_v, mla_v)

    @pl.when(is_b & (chip > 1))
    def _():
        for group in groups:
            take_state(MAP_G, group)
            send_state(MAP_Y, group)

    latent_finish(half, half, scores[1], keys, up_v, mla_v)

    @pl.when(is_b & (chip > 1))
    def _():
        for group in groups:
            emit(group, [recv_buf[MAP_G, h] for h in members(group)])

    @pl.when(is_a & (chip > 1))
    def _():
        for group in groups:
            emit(group, take_state(MAP_Y, group))

    for i in range(2):
        @pl.when(shard + near[i] < shards)
        def _(i=i):
            near_copy(i).wait_send()

        twin_copy(i).wait_send()
    for i in range(SPAN // 2 + 1):
        for step in range(1, head_devices):
            side_copy(i, step, side).wait_send()
    for kind, condition in sends.items():
        @pl.when(condition)
        def _(kind=kind):
            for group in groups:
                state_copy(kind, group).wait_send()


def write_out(delta_ref, mla_ref, delta_hbm, mla_hbm, sem):
    copies = []
    for source, target in ((delta_ref, delta_hbm), (mla_ref, mla_hbm)):
        step = source.shape[0] // PIECES
        for i in range(PIECES):
            part = pl.ds(i * step, step)
            copies.append(
                pltpu.make_async_copy(source.at[part], target.at[part], sem.at[len(copies)])
            )
    for copy in copies:
        copy.start()
    for copy in copies:
        copy.wait()


def solution(mesh):
    shards = mesh.shape["context"]
    head_devices = mesh.shape["head"]

    def step(query_vec, key_vec, value_vec, log_decay, beta, latent, latent_query, w_uv, doc_lengths):
        rows = query_vec.shape[0]
        heads = beta.shape[1]
        rank = w_uv.shape[0]
        width = query_vec.shape[1]
        keys = (SPAN + 1) * rows
        square = (rows, rows)
        outside = pl.BlockSpec(memory_space=pltpu.HBM)
        inside = pl.BlockSpec(memory_space=pltpu.VMEM)
        dma = pltpu.SemaphoreType.DMA
        side_copies = (SPAN // 2 + 1) * (head_devices - 1)
        inputs = (query_vec, key_vec, value_vec, log_decay, beta.T, latent, latent_query, w_uv, doc_lengths.reshape(1, -1))
        inputs = [pltpu.with_memory_space_constraint(x, pltpu.HBM) for x in inputs]
        delta, mla = pl.pallas_call(
            functools.partial(body, shards, head_devices, heads, WIDTH**-0.5),
            out_shape=(
                jax.ShapeDtypeStruct((rows, width), F32),
                jax.ShapeDtypeStruct((rows, width), BF16),
            ),
            in_specs=[outside] * 9,
            out_specs=(inside, inside),
            scratch_shapes=[
                pltpu.VMEM((rows, width), F32),
                pltpu.VMEM((rows, width), F32),
                pltpu.VMEM((rows, width), F32),
                pltpu.VMEM((rows, width), F32),
                pltpu.VMEM((heads, rows), F32),
                pltpu.VMEM((rows * heads, rank), BF16),
                pltpu.VMEM((rank, width), BF16),
                pltpu.VMEM((keys, rank), BF16),
                pltpu.VMEM((1, doc_lengths.shape[0]), jnp.int32),
                pltpu.VMEM((2,) + square, F32),
                pltpu.VMEM((2,) + square, F32),
                pltpu.VMEM((LEVELS + 1,) + square, BF16),
                pltpu.VMEM((rows, keys), F32),
                pltpu.VMEM((heads,) + square, BF16),
                pltpu.VMEM((heads,) + square, F32),
                pltpu.VMEM((heads,) + square, BF16),
                pltpu.VMEM((heads,) + square, BF16),
                pltpu.VMEM((6, heads) + square, BF16),
                pltpu.VMEM((6, heads) + square, BF16),
                dma((8 + heads,)),
                dma((6, heads // BATCH)),
                dma((6, heads // BATCH)),
                dma((2,)),
                dma((2,)),
                dma((side_copies,)),
                dma((side_copies,)),
                dma((2,)),
                dma((2,)),
            ],
            compiler_params=pltpu.CompilerParams(
                collective_id=0, has_side_effects=True, vmem_limit_bytes=48 * 1024 * 1024
            ),
            cost_estimate=pl.CostEstimate(flops=3_000_000_000, bytes_accessed=6_000_000, transcendentals=1_000_000),
            name="packed_attention",
        )(*inputs)
        anywhere = pl.BlockSpec(memory_space=pl.ANY)
        return pl.pallas_call(
            write_out,
            out_shape=(
                jax.ShapeDtypeStruct((rows, width), F32),
                jax.ShapeDtypeStruct((rows, width), BF16),
            ),
            in_specs=[anywhere, anywhere],
            out_specs=(pl.BlockSpec(memory_space=pltpu.HBM), pl.BlockSpec(memory_space=pltpu.HBM)),
            scratch_shapes=[dma((2 * PIECES,))],
            compiler_params=pltpu.CompilerParams(vmem_limit_bytes=1024 * 1024),
            name="write_out",
        )(delta, mla)

    return jax.shard_map(
        step,
        mesh=mesh,
        in_specs=(
            P("context", "head"),
            P("context", "head"),
            P("context", "head"),
            P("context", "head"),
            P("context", "head"),
            P(("context", "head"), None),
            P("context", "head"),
            P(None, "head"),
            P(),
        ),
        out_specs=(P("context", "head"), P("context", "head")),
        check_vma=False,
    )
```

```python
import functools

import jax
import jax.numpy as jnp
from jax import lax
from jax.experimental import pallas as pl
from jax.experimental.pallas import tpu as pltpu
from jax.sharding import PartitionSpec as P

MESH = pl.DeviceIdType.MESH
F32 = jnp.float32
BF16 = jnp.bfloat16
FAR = -1e30
EPS = 1e-6
SPAN = 4
TOK = 128
WIDTH = 128
LEVELS = 7
BATCH = 2
PIECES = 2


def mul(left, right):
    return lax.dot_general(left, right, (((1,), (0,)), ((), ())), preferred_element_type=F32)


def mul_nt(left, right):
    return lax.dot_general(left, right, (((1,), (1,)), ((), ())), preferred_element_type=F32)


def halves(matrix):
    high = matrix.astype(BF16)
    return high, (matrix - high.astype(F32)).astype(BF16)


def three(product, left, right):
    return product(left[0], right[0]) + product(left[1], right[0]) + product(left[0], right[1])


def iota2(shape, axis):
    return lax.broadcasted_iota(jnp.int32, shape, axis)


def prepare_masks(lens, shard, pair_mask, link_mask, level_mask):
    square = (TOK, TOK)
    row, col = iota2(square, 0), iota2(square, 1)
    lens_f = lens.astype(F32)
    lens_row = jnp.broadcast_to(lens_f, square)
    begin_col = jnp.sum(jnp.where(col < row, lens_row, 0.0), axis=1, keepdims=True)
    lens_col = jnp.sum(jnp.where(col == row, lens_row, 0.0), axis=1, keepdims=True)
    begin_row = jnp.sum(jnp.where(row < col, lens_col, 0.0), axis=0, keepdims=True)
    low = shard * TOK
    pos_col = (low + iota2((TOK, 1), 0)).astype(F32)
    start_col = jnp.max(jnp.where(begin_row <= pos_col, begin_row, -1.0), axis=1, keepdims=True)
    pos_row = (low + iota2((1, TOK), 1)).astype(F32)
    start_row = jnp.max(jnp.where(begin_col <= pos_row, begin_col, -1.0), axis=0, keepdims=True)
    same = start_col == start_row
    pair_mask[0] = jnp.where(same & (row >= col), 1.0, 0.0)
    pair_mask[1] = jnp.where(same & (row > col), 1.0, 0.0)
    link_mask[0] = jnp.broadcast_to(jnp.where(start_col < low.astype(F32), 1.0, 0.0), square)
    link_mask[1] = jnp.broadcast_to(jnp.where(start_col == start_col[TOK - 1 :, :], 1.0, 0.0), square)
    for level in range(LEVELS):
        below = ((row >> (level + 1)) == (col >> (level + 1))) & ((row >> level) > (col >> level))
        level_mask[level] = jnp.where(below, 1.0, 0.0).astype(BF16)
    level_mask[LEVELS] = jnp.where(row == col, 1.0, 0.0).astype(BF16)
    return begin_col, start_col, pos_col


def prepare_bias(found, shard, bias):
    begin_col, start_col, pos_col = found
    keys = (SPAN + 1) * TOK
    pos_row = ((shard - SPAN) * TOK + iota2((1, keys), 1)).astype(F32)
    start_row = jnp.max(jnp.where(begin_col <= pos_row, begin_col, -1.0), axis=0, keepdims=True)
    visible = (start_col == start_row) & (pos_row <= pos_col)
    bias[...] = jnp.where(visible, 0.0, FAR)


def delta_pairs(heads, refs, pair_mask, link_mask):
    key_ref, value_ref, decay_ref, beta_ref = refs
    square = (TOK, TOK)
    row, col = iota2(square, 0), iota2(square, 1)
    lower = jnp.where(row >= col, 1.0, 0.0).astype(BF16)
    strict = pair_mask[1] > 0.5
    link, tail = link_mask[0], link_mask[1]
    link_last = link[TOK - 1 :, :]
    beta_cols = beta_ref[...].T
    parts = []
    for h in range(heads):
        lanes = slice(h * WIDTH, (h + 1) * WIDTH)
        decay = decay_ref[:, lanes]
        high = decay.astype(BF16)
        rest = decay - high.astype(F32)
        mid = rest.astype(BF16)
        low = (rest - mid.astype(F32)).astype(BF16)
        cum = mul(lower, high) + mul(lower, mid) + mul(lower, low)
        centre, end = cum[TOK // 2 - 1 : TOK // 2, :], cum[TOK - 1 :, :]
        grow, shrink = jnp.exp(cum - centre), jnp.exp(centre - cum)
        from_start, to_end = jnp.exp(centre), jnp.exp(end - centre)
        key = key_ref[:, lanes]
        key = key * lax.rsqrt(jnp.sum(key * key, axis=1, keepdims=True) + EPS)
        key_grow, key_shrink = key * grow, key * shrink
        shrunk = halves(key_shrink)
        pairs = three(mul_nt, halves(key_grow), shrunk)
        beta = beta_cols[:, h : h + 1]
        in_scale = link * from_start
        parts.append(
            dict(
                grow=grow,
                shrunk=shrunk,
                in_scale=in_scale,
                system=halves(jnp.where(strict, pairs, 0.0) * beta),
                right=jnp.concatenate(
                    [value_ref[:, lanes] * beta, key_grow * in_scale * beta], axis=1
                ),
                tail=halves((key_shrink * (tail * to_end)).T),
                end=jnp.exp(end) * link_last,
            )
        )
    return parts


def delta_solve(parts, level_mask, a_ref, c_ref, midway, finished):
    square = (TOK, TOK)
    row, col = iota2(square, 0), iota2(square, 1)
    system = [part["system"] for part in parts]
    right = [part["right"] for part in parts]
    span = range(len(parts))
    inverse = [level_mask[LEVELS] - system[h][0] * level_mask[0] for h in span]
    for level in range(1, LEVELS):
        if level == 1:
            midway()
        inner = [mul(system[h][0] * level_mask[level], inverse[h]).astype(BF16) for h in span]
        inverse = [inverse[h] - mul(inverse[h], inner[h]).astype(BF16) for h in span]
    solved = [mul(inverse[h], right[h].astype(BF16)) for h in span]
    rest = [right[h] - solved[h] - three(mul, system[h], halves(solved[h])) for h in span]
    solved = [halves(solved[h] + mul(inverse[h], rest[h].astype(BF16))) for h in span]
    for group in range(len(parts) // BATCH):
        for h in range(group * BATCH, (group + 1) * BATCH):
            change = three(mul, parts[h]["tail"], solved[h])
            c_ref[h] = change[:, :WIDTH]
            a_ref[h] = (jnp.where(row == col, parts[h]["end"], 0.0) - change[:, WIDTH:]).astype(BF16)
        finished(group)
    return solved


def delta_outputs(parts, solved, query_ref, pair_mask, left_ref, base_ref):
    incl = pair_mask[0] > 0.5
    for h, part in enumerate(parts):
        lanes = slice(h * WIDTH, (h + 1) * WIDTH)
        query = query_ref[:, lanes]
        query = query * lax.rsqrt(jnp.sum(query * query, axis=1, keepdims=True) + EPS)
        query = query * part["grow"]
        weight = jnp.where(incl, three(mul_nt, halves(query), part["shrunk"]), 0.0)
        output = three(mul, halves(weight), solved[h])
        base_ref[:, lanes] = output[:, :WIDTH]
        left_ref[h] = (query * part["in_scale"] - output[:, WIDTH:]).astype(BF16)


def latent_scores(first, heads, scale, query_rows, keys, bias):
    rows = query_rows[first * TOK : (first + heads) * TOK, :]
    return mul_nt(rows, keys[...]) * scale + jnp.concatenate([bias[...]] * heads, axis=0)


def latent_finish(first, heads, scores, keys, up_ref, out_ref):
    top = jnp.max(scores, axis=1, keepdims=True)
    weights = jnp.exp(scores - top)
    totals = jnp.sum(weights, axis=1, keepdims=True)
    context = mul(weights.astype(BF16), keys[...]) * (1.0 / totals)
    context = context.astype(BF16)
    for h in range(heads):
        at = (first + h) * WIDTH
        out_ref[:, at : at + WIDTH] = mul(
            context[h * TOK : (h + 1) * TOK], up_ref[:, at : at + WIDTH]
        ).astype(BF16)


def body(
    shards, head_devices, heads, scale,
    query_hbm, key_hbm, value_hbm, decay_hbm, beta_hbm, latent_hbm, latq_hbm, up_hbm, lens_hbm,
    base, mla_v,
    query_v, key_v, value_v, decay_v, beta_v, latq_v, up_v, keys, lens_v,
    pair_mask, link_mask, level_mask, bias,
    a_ref, c_ref, left_ref, step_ref, send_buf, recv_buf,
    load_sem, chain_send, chain_recv, near_send, near_recv, side_send, side_recv, twin_send, twin_recv,
):
    shard = lax.axis_index("context")
    side = lax.axis_index("head")
    core = lax.rem(shard, 2)
    chip = shard // 2
    last = shards // 2 - 1
    is_a, is_b = core == 0, core == 1
    rank = latq_v.shape[1]
    quarter = TOK // head_devices
    near = (2, 4)
    batch = BATCH

    def ahead(steps):
        return lax.rem(shard + shards + steps, shards)

    def block_rows(block, place):
        return pl.ds(pl.multiple_of(block * TOK + place * quarter, quarter), quarter)

    pairs = [(lens_hbm, lens_v), (decay_hbm, decay_v), (key_hbm, key_v), (beta_hbm, beta_v)]
    pairs += [(value_hbm, value_v), (query_hbm, query_v), (up_hbm, up_v)]
    pairs += [
        (latq_hbm.at[:, pl.ds(h * rank, rank)], latq_v.at[pl.ds(h * TOK, TOK), :]) for h in range(heads)
    ]
    pairs += [(latent_hbm, keys.at[block_rows(SPAN, side)])]
    loads = [pltpu.make_async_copy(pairs[i][0], pairs[i][1], load_sem.at[i]) for i in range(len(pairs))]
    loads[0].start()
    loads[-1].start()
    for load in loads[1:-1]:
        load.start()

    barrier = pltpu.get_barrier_semaphore()

    def greet(peer):
        pl.semaphore_signal(barrier, inc=1, device_id=peer, device_id_type=MESH)

    for step in range(1, head_devices):
        greet((shard, lax.rem(side + step, head_devices)))
    greet((shard + 1 - 2 * core, side))
    for steps in near:
        @pl.when(shard >= steps)
        def _(steps=steps):
            greet((ahead(-steps), side))

    def one_if(condition):
        return jnp.where(condition, 1, 0).astype(jnp.int32)

    expected = head_devices
    for steps in near:
        expected = expected + one_if(shard + steps < shards)

    def near_copy(i):
        return pltpu.make_async_remote_copy(
            src_ref=latent_hbm, dst_ref=keys.at[block_rows(SPAN - near[i], side)],
            send_sem=near_send.at[i], recv_sem=near_recv.at[i],
            device_id=(ahead(near[i]), side), device_id_type=MESH,
        )

    def side_copy(i, step, place):
        rows = block_rows(SPAN - 2 * i, place)
        at = i * (head_devices - 1) + step - 1
        return pltpu.make_async_remote_copy(
            src_ref=keys.at[rows], dst_ref=keys.at[rows],
            send_sem=side_send.at[at], recv_sem=side_recv.at[at],
            device_id=(shard, lax.rem(side + step, head_devices)), device_id_type=MESH,
        )

    def side_start(i):
        for step in range(1, head_devices):
            side_copy(i, step, side).start()

    def side_arrived(i):
        for step in range(1, head_devices):
            side_copy(i, step, lax.rem(side + head_devices - step, head_devices)).wait_recv()

    def twin_copy(i):
        source = pl.ds(pl.multiple_of((2 * i + 2 * (1 - core)) * TOK, TOK), TOK)
        return pltpu.make_async_remote_copy(
            src_ref=keys.at[source], dst_ref=keys.at[pl.ds((2 * i + 1) * TOK, TOK)],
            send_sem=twin_send.at[i], recv_sem=twin_recv.at[i],
            device_id=(shard + 1 - 2 * core, side), device_id_type=MESH,
        )

    MAP_C, MAP_A, MAP_D, MAP_G, MAP_X, MAP_Y = range(6)
    jump = {MAP_C: 1, MAP_A: 1, MAP_D: 2, MAP_G: 2, MAP_X: -1, MAP_Y: -1}

    def state_copy(kind, group):
        part = pl.ds(group * batch, batch)
        if kind == MAP_A:
            source = a_ref.at[part]
        elif kind in (MAP_X, MAP_Y):
            source = recv_buf.at[MAP_D if kind == MAP_X else MAP_G, part]
        else:
            source = send_buf.at[kind, part]
        return pltpu.make_async_remote_copy(
            src_ref=source, dst_ref=recv_buf.at[kind, part],
            send_sem=chain_send.at[kind, group], recv_sem=chain_recv.at[kind, group],
            device_id=(ahead(jump[kind]), side), device_id_type=MESH,
        )

    def members(group):
        return range(group * batch, (group + 1) * batch)

    def send_state(kind, group, values=None):
        if values is not None:
            for h, value in zip(members(group), values):
                send_buf[kind, h] = value.astype(BF16)
        state_copy(kind, group).start()

    def take_state(kind, group):
        state_copy(kind, group).wait_recv()
        return [recv_buf[kind, h] for h in members(group)]

    sends = {
        MAP_C: is_a,
        MAP_A: is_a,
        MAP_D: is_b & (chip < last),
        MAP_G: is_b & (chip > 0) & (chip < last),
        MAP_X: is_b & (chip > 0),
        MAP_Y: is_b & (chip > 1),
    }
    groups = range(heads // batch)

    def emit(group, incoming):
        for h, state in zip(members(group), incoming):
            lanes = slice(h * WIDTH, (h + 1) * WIDTH)
            base[:, lanes] += mul(left_ref[h], state)

    loads[0].wait()
    found = prepare_masks(lens_v[...], shard, pair_mask, link_mask, level_mask)
    for load in loads[1:5]:
        load.wait()
    parts = delta_pairs(heads, (key_v, value_v, decay_v, beta_v), pair_mask, link_mask)

    def open_links():
        pl.semaphore_wait(barrier, expected)
        for i in range(2):
            @pl.when(shard + near[i] < shards)
            def _(i=i):
                near_copy(i).start()
        loads[-1].wait()
        side_start(0)

    def send_maps(group):
        @pl.when(is_a)
        def _():
            send_state(MAP_C, group, [c_ref[h] for h in members(group)])

    solved = delta_solve(parts, level_mask, a_ref, c_ref, open_links, send_maps)

    @pl.when(is_a)
    def _():
        for group in groups:
            send_state(MAP_A, group)

    loads[5].wait()
    delta_outputs(parts, solved, query_v, pair_mask, left_ref, base)

    @pl.when(is_b & (chip < last))
    def _():
        for group in groups:
            incoming = take_state(MAP_C, group)
            send_state(
                MAP_D, group, [c_ref[h] + mul(a_ref[h], x) for h, x in zip(members(group), incoming)]
            )

    @pl.when(is_b & (chip == last))
    def _():
        for group in groups:
            take_state(MAP_C, group)

    @pl.when(is_b)
    def _():
        for group in groups:
            incoming = take_state(MAP_A, group)
            emit(group, [recv_buf[MAP_C, h] for h in members(group)])
            for h, x in zip(members(group), incoming):
                step_ref[h] = mul(a_ref[h], x).astype(BF16)
                left_ref[h] = mul(left_ref[h], x).astype(BF16)

    for i in range(2):
        @pl.when(shard >= near[i])
        def _(i=i):
            near_copy(i).wait_recv()

        @pl.when(shard < near[i])
        def _(i=i):
            keys[block_rows(SPAN - near[i], side), :] = jnp.zeros((quarter, rank), BF16)

        side_start(i + 1)

    @pl.when(is_b & (chip > 0) & (chip < last))
    def _():
        for group in groups:
            incoming = take_state(MAP_D, group)
            send_state(MAP_G, group, [mul(step_ref[h], x) for h, x in zip(members(group), incoming)])
            send_state(MAP_X, group)

    @pl.when(is_b & (chip == last))
    def _():
        for group in groups:
            take_state(MAP_D, group)
            send_state(MAP_X, group)

    prepare_bias(found, shard, bias)

    side_arrived(0)

    @pl.when(is_a)
    def _():
        twin_copy(1).start()

    side_arrived(1)

    @pl.when(is_a)
    def _():
        twin_copy(0).start()

    @pl.when(is_b)
    def _():
        twin_copy(1).start()

    side_arrived(2)

    @pl.when(is_b)
    def _():
        twin_copy(0).start()

    @pl.when(is_a & (chip > 0))
    def _():
        for group in groups:
            emit(group, take_state(MAP_X, group))

    @pl.when(is_b & (chip > 0))
    def _():
        for group in groups:
            emit(group, [recv_buf[MAP_D, h] for h in members(group)])

    for load in loads[6:-1]:
        load.wait()
    for i in range(2):
        twin_copy(i).wait_recv()

    half = heads // 2
    scores = [latent_scores(part * half, half, scale, latq_v, keys, bias) for part in range(2)]
    latent_finish(0, half, scores[0], keys, up_v, mla_v)

    @pl.when(is_b & (chip > 1))
    def _():
        for group in groups:
            take_state(MAP_G, group)
            send_state(MAP_Y, group)

    latent_finish(half, half, scores[1], keys, up_v, mla_v)

    @pl.when(is_b & (chip > 1))
    def _():
        for group in groups:
            emit(group, [recv_buf[MAP_G, h] for h in members(group)])

    @pl.when(is_a & (chip > 1))
    def _():
        for group in groups:
            emit(group, take_state(MAP_Y, group))

    for i in range(2):
        @pl.when(shard + near[i] < shards)
        def _(i=i):
            near_copy(i).wait_send()

        twin_copy(i).wait_send()
    for i in range(SPAN // 2 + 1):
        for step in range(1, head_devices):
            side_copy(i, step, side).wait_send()
    for kind, condition in sends.items():
        @pl.when(condition)
        def _(kind=kind):
            for group in groups:
                state_copy(kind, group).wait_send()


def write_out(delta_ref, mla_ref, delta_hbm, mla_hbm, sem):
    copies = []
    for source, target in ((delta_ref, delta_hbm), (mla_ref, mla_hbm)):
        step = source.shape[0] // PIECES
        for i in range(PIECES):
            part = pl.ds(i * step, step)
            copies.append(
                pltpu.make_async_copy(source.at[part], target.at[part], sem.at[len(copies)])
            )
    for copy in copies:
        copy.start()
    for copy in copies:
        copy.wait()


def solution(mesh):
    shards = mesh.shape["context"]
    head_devices = mesh.shape["head"]

    def step(query_vec, key_vec, value_vec, log_decay, beta, latent, latent_query, w_uv, doc_lengths):
        rows = query_vec.shape[0]
        heads = beta.shape[1]
        rank = w_uv.shape[0]
        width = query_vec.shape[1]
        keys = (SPAN + 1) * rows
        square = (rows, rows)
        outside = pl.BlockSpec(memory_space=pltpu.HBM)
        inside = pl.BlockSpec(memory_space=pltpu.VMEM)
        dma = pltpu.SemaphoreType.DMA
        side_copies = (SPAN // 2 + 1) * (head_devices - 1)
        inputs = (query_vec, key_vec, value_vec, log_decay, beta.T, latent, latent_query, w_uv, doc_lengths.reshape(1, -1))
        inputs = [pltpu.with_memory_space_constraint(x, pltpu.HBM) for x in inputs]
        delta, mla = pl.pallas_call(
            functools.partial(body, shards, head_devices, heads, WIDTH**-0.5),
            out_shape=(
                jax.ShapeDtypeStruct((rows, width), F32),
                jax.ShapeDtypeStruct((rows, width), BF16),
            ),
            in_specs=[outside] * 9,
            out_specs=(inside, inside),
            scratch_shapes=[
                pltpu.VMEM((rows, width), F32),
                pltpu.VMEM((rows, width), F32),
                pltpu.VMEM((rows, width), F32),
                pltpu.VMEM((rows, width), F32),
                pltpu.VMEM((heads, rows), F32),
                pltpu.VMEM((rows * heads, rank), BF16),
                pltpu.VMEM((rank, width), BF16),
                pltpu.VMEM((keys, rank), BF16),
                pltpu.VMEM((1, doc_lengths.shape[0]), jnp.int32),
                pltpu.VMEM((2,) + square, F32),
                pltpu.VMEM((2,) + square, F32),
                pltpu.VMEM((LEVELS + 1,) + square, BF16),
                pltpu.VMEM((rows, keys), F32),
                pltpu.VMEM((heads,) + square, BF16),
                pltpu.VMEM((heads,) + square, F32),
                pltpu.VMEM((heads,) + square, BF16),
                pltpu.VMEM((heads,) + square, BF16),
                pltpu.VMEM((6, heads) + square, BF16),
                pltpu.VMEM((6, heads) + square, BF16),
                dma((8 + heads,)),
                dma((6, heads // BATCH)),
                dma((6, heads // BATCH)),
                dma((2,)),
                dma((2,)),
                dma((side_copies,)),
                dma((side_copies,)),
                dma((2,)),
                dma((2,)),
            ],
            compiler_params=pltpu.CompilerParams(
                collective_id=0, has_side_effects=True, vmem_limit_bytes=48 * 1024 * 1024
            ),
            cost_estimate=pl.CostEstimate(flops=3_000_000_000, bytes_accessed=6_000_000, transcendentals=1_000_000),
            name="packed_attention",
        )(*inputs)
        anywhere = pl.BlockSpec(memory_space=pl.ANY)
        return pl.pallas_call(
            write_out,
            out_shape=(
                jax.ShapeDtypeStruct((rows, width), F32),
                jax.ShapeDtypeStruct((rows, width), BF16),
            ),
            in_specs=[anywhere, anywhere],
            out_specs=(pl.BlockSpec(memory_space=pltpu.HBM), pl.BlockSpec(memory_space=pltpu.HBM)),
            scratch_shapes=[dma((2 * PIECES,))],
            compiler_params=pltpu.CompilerParams(vmem_limit_bytes=1024 * 1024),
            name="write_out",
        )(delta, mla)

    return jax.shard_map(
        step,
        mesh=mesh,
        in_specs=(
            P("context", "head"),
            P("context", "head"),
            P("context", "head"),
            P("context", "head"),
            P("context", "head"),
            P(("context", "head"), None),
            P("context", "head"),
            P(None, "head"),
            P(),
        ),
        out_specs=(P("context", "head"), P("context", "head")),
        check_vma=False,
    )
```
